256 devices in a mesh: dp: 64 (over y, x, z_hi), tensor: 4 (over z_lo, core).
Axes of the slice: x: 4, y: 4, z: 8 (z_hi: 4, z_lo: 2; z = z_hi * 2 + z_lo), core: 2. Of those that a mesh axis runs over, the one named last changes fastest.
Arguments:
- inputs: bfloat16 [7168, 128], P('dp'), may hold values from -6 to 6
- ln_gain: float32 [7168], P('dp'), may hold values from 0.5 to 1.5
- segment_ids: int32 [128], replicated, may hold values from 0 to 7, never falling along the last dimension, each value on 1 to 32 neighbouring positions
- w_in: bfloat16 [7168, 14336], P('dp', 'tensor'), may hold values from -0.0625 to 0.0625
- w_out: bfloat16 [7168, 14336], P('dp', 'tensor'), may hold values from -0.046875 to 0.046875
- mom_in: bfloat16 [7168, 14336], P('dp', 'tensor'), may hold values from -0.119628906 to 0.119628906
- mom_out: bfloat16 [7168, 14336], P('dp', 'tensor'), may hold values from -0.119628906 to 0.119628906
- hess_in: bfloat16 [7168, 14336], P('dp', 'tensor'), may hold values from 0.0099487305 to 1
- hess_out: bfloat16 [7168, 14336], P('dp', 'tensor'), may hold values from 0.0099487305 to 1
- probe_seed: int32 [2], replicated, may hold values from 0 to 1073741823
Outputs:
- new_mom_in: bfloat16 [7168, 14336], P('dp', 'tensor')
- new_hess_in: bfloat16 [7168, 14336], P('dp', 'tensor')
- step_in: bfloat16 [7168, 14336], P('dp', 'tensor')
- new_mom_out: bfloat16 [7168, 14336], P('dp', 'tensor')
- new_hess_out: bfloat16 [7168, 14336], P('dp', 'tensor')
- step_out: bfloat16 [7168, 14336], P('dp', 'tensor')
The draws below stay inside these ranges and needn't reach their ends.
Inputs may be any that keep to these rules, and one draw needn't show every extreme that they name: `segment_ids`: document numbers never fall along the tokens; each document has at most 32 tokens, and one has exactly that many.
All inputs are finite; a program needn't handle non-finite values.
Results may differ from the reference program's by a relative error of at most 0.039.
Values may be sent and summed in bfloat16 or wider, within the bound.
No kernel may reach another device: no remote copies, remote signals or barrier semaphores. Data moves between devices by JAX's collectives and lax.ppermute only.
A program may use at most 64 MiB of HBM per device.

```python
import math
import jax
import jax.numpy as jnp
import numpy as np
from jax import lax

D = 7168
FF = 14336
TOKENS = 128
DOCS = 8
DOC_MOST = 32


def shard_levels(key, shape, cuts, smallest, largest):
    level, own = 1.0, jax.random.fold_in(key, 6)
    for axis_at, parts in cuts:
        steps = jnp.exp(jax.random.uniform(jax.random.fold_in(own, axis_at), (parts,), jnp.float32, smallest / len(cuts), largest / len(cuts)))
        level = level * jnp.repeat(steps, shape[axis_at] // parts).reshape([-1 if axis == axis_at else 1 for axis in range(len(shape))])
    return level


def split_up(amount, total, limit, lean):
    weights = [(1 << 20) // math.isqrt(rank ** lean) + 1 for rank in range(2, amount + 1)]
    rest, holding = total - limit - (amount - 1), [1] * (amount - 1)
    while rest > 0:
        movable = [i for i in range(amount - 1) if holding[i] < limit]
        whole, remaining = sum([weights[i] for i in movable]), rest
        for i in movable:
            extra = min(limit - holding[i], max(1, remaining * weights[i] // whole), rest)
            holding[i] = holding[i] + extra
            rest = rest - extra
    return np.array([limit] + holding)


def uneven(key, number_of, total, bound, skew):
    if number_of == 2:
        one = jax.random.randint(key, (), max(1, total - bound), min(bound, total - 1) + 1)
        return jnp.stack([one, total - one])
    sizes = jnp.asarray(split_up(number_of, total, bound, skew), jnp.int32)
    twos = (number_of - 1) // 2
    source_of, sink = sizes[1:1 + 2 * twos:2], sizes[2:2 + 2 * twos:2]
    room = jnp.minimum(source_of - 1, bound - sink)
    moved = jax.random.randint(jax.random.fold_in(key, 1), (twos,), 0, 1 << 20) % (room + 1)
    sizes = sizes.at[1:1 + 2 * twos:2].set(source_of - moved).at[2:2 + 2 * twos:2].set(sink + moved)
    return sizes[jax.random.permutation(jax.random.fold_in(key, 2), number_of)]


def centred(rng, dims, deviation, reach, shards=(), held_as=jnp.bfloat16):
    values = jax.random.normal(rng, dims, jnp.float32) * deviation
    if len(shards) > 0:
        values = shard_levels(rng, dims, shards, -0.22, 0.18) * values
    return jnp.clip(values, min=-reach, max=reach).astype(held_as)


def setup_inputs(seed: int = 0) -> dict:
    streams_of = jax.random.split(jax.random.key(seed), 11)
    return {
        "inputs": centred(streams_of[0], (D, TOKENS), 1.0, 6.0, ((0, 64),)),
        "ln_gain": jnp.clip(1.0 + 0.1 * jax.random.normal(streams_of[1], (D,), jnp.float32), 0.5, 1.5),
        "segment_ids": jnp.searchsorted(jnp.cumsum(uneven(streams_of[2], DOCS, TOKENS, DOC_MOST, 1)), jnp.arange(TOKENS), side="right").astype(jnp.int32),
        "w_in": centred(streams_of[3], (D, FF), D ** -0.5, 0.0625, ((0, 64), (1, 4))),
        "w_out": centred(streams_of[4], (D, FF), FF ** -0.5, 0.046875, ((0, 64), (1, 4))),
        "mom_in": centred(streams_of[5], (D, FF), 0.02, 0.119628906, ((0, 64), (1, 4))),
        "mom_out": centred(streams_of[6], (D, FF), 0.02, 0.119628906, ((0, 64), (1, 4))),
        "hess_in": jnp.clip(jnp.exp(math.log(1.0) - 4.61031033 * jax.random.uniform(streams_of[7], (D, FF), jnp.float32) ** shard_levels(streams_of[7], (D, FF), ((0, 64), (1, 4)), -0.2, 0.2)), 0.0099487305, 1.0).astype(jnp.bfloat16),
        "hess_out": jnp.clip(jnp.exp(math.log(1.0) - 4.61031033 * jax.random.uniform(streams_of[8], (D, FF), jnp.float32) ** shard_levels(streams_of[8], (D, FF), ((0, 64), (1, 4)), -0.2, 0.2)), 0.0099487305, 1.0).astype(jnp.bfloat16),
        "probe_seed": jax.random.randint(streams_of[9], (2,), 0, 1073741824).astype(jnp.int32),
    }


BETA_ONE = 0.96
BETA_TWO = 0.99
SCALE_GAMMA = 0.05
FLOOR_EPS = 0.002
NORM_EPS = 1e-05
hash_factor = 73244475

def mixing(words):
    words = (words ^ words >> 16 & 65535) * hash_factor
    words = (words ^ words >> 16 & 65535) * hash_factor
    return words ^ words >> 16 & 65535

def probe_signs(seed_word, row_start, col_start, row_count, col_count, total_cols):
    rows_index = row_start + jnp.arange(row_count, dtype=jnp.int32)[:, None]
    cols_index = col_start + jnp.arange(col_count, dtype=jnp.int32)[None, :]
    hashed = mixing(rows_index * total_cols + cols_index ^ seed_word)
    return (1 - 2 * (hashed & 1)).astype(jnp.bfloat16)

def full_probe(seed_word):
    block_rows = math.gcd(D, 128)

    def one_block(block_index):
        return probe_signs(seed_word, block_index * block_rows, 0, block_rows, FF, FF)
    pieces = lax.map(one_block, jnp.arange(D // block_rows, dtype=jnp.int32))
    return pieces.reshape(D, FF)

def gelu_parts(preact):
    normal_cdf = 0.5 * (1.0 + lax.erf(preact * 0.7071067811865476))
    normal_pdf = jnp.exp(-0.5 * preact * preact) * 0.3989422804014327
    return (preact * normal_cdf, normal_cdf + preact * normal_pdf, normal_pdf * (2.0 - preact * preact))

def token_weights(segment_ids):
    following = jnp.concatenate([segment_ids[1:], jnp.full((1,), -1, jnp.int32)])
    valid = (following == segment_ids).astype(jnp.float32)
    same_doc = (segment_ids[:, None] == segment_ids[None, :]).astype(jnp.float32)
    counts = jnp.dot(same_doc, valid, precision=lax.Precision.HIGHEST)
    return valid / jnp.maximum(counts, 1.0)

def sophia_update(moment_old, curve_old, gradient, product, probe):
    moment = BETA_ONE * moment_old.astype(jnp.float32) + (1.0 - BETA_ONE) * gradient
    curvature = BETA_TWO * curve_old.astype(jnp.float32) + (1.0 - BETA_TWO) * probe.astype(jnp.float32) * product
    stepped = jnp.clip(moment / jnp.maximum(SCALE_GAMMA * curvature, FLOOR_EPS), -1.0, 1.0)
    return (moment.astype(jnp.bfloat16), curvature.astype(jnp.bfloat16), stepped.astype(jnp.bfloat16))

def reference(inputs, ln_gain, segment_ids, w_in, w_out, mom_in, mom_out, hess_in, hess_out, probe_seed):
    values = inputs.astype(jnp.float32)
    mean_val = lax.optimization_barrier(jnp.mean(values, axis=0))
    centered = values - mean_val
    variance = lax.optimization_barrier(jnp.mean(centered * centered, axis=0))
    normed = (centered * lax.rsqrt(variance + NORM_EPS) * ln_gain[:, None]).astype(jnp.bfloat16)
    probe_in = full_probe(probe_seed[0])
    probe_out = full_probe(probe_seed[1])
    rows_first = normed.T
    preact = jnp.dot(rows_first, w_in, preferred_element_type=jnp.float32)
    preact_dot = jnp.dot(rows_first, probe_in, preferred_element_type=jnp.float32)
    hidden_full, slope, curve = gelu_parts(preact)
    hidden = hidden_full.astype(jnp.bfloat16)
    hidden_dot = (slope * preact_dot).astype(jnp.bfloat16)
    output = jnp.dot(w_out, hidden.T, preferred_element_type=jnp.float32)
    output_dot = jnp.dot(w_out, hidden_dot.T, preferred_element_type=jnp.float32) + jnp.dot(probe_out, hidden.T, preferred_element_type=jnp.float32)
    target = jnp.concatenate([values[:, 1:], jnp.zeros((values.shape[0], 1), jnp.float32)], axis=1)
    weights = token_weights(segment_ids)
    cotangent = (weights * (output - target)).astype(jnp.bfloat16)
    cotangent_dot = (weights * output_dot).astype(jnp.bfloat16)
    grad_out = jnp.dot(cotangent, hidden, preferred_element_type=jnp.float32)
    hvp_out = jnp.dot(cotangent_dot, hidden, preferred_element_type=jnp.float32) + jnp.dot(cotangent, hidden_dot, preferred_element_type=jnp.float32)
    back = jnp.dot(cotangent.T, w_out, preferred_element_type=jnp.float32)
    back_dot = jnp.dot(cotangent_dot.T, w_out, preferred_element_type=jnp.float32) + jnp.dot(cotangent.T, probe_out, preferred_element_type=jnp.float32)
    pre_grad = (slope * back).astype(jnp.bfloat16)
    pre_grad_dot = (curve * preact_dot * back + slope * back_dot).astype(jnp.bfloat16)
    grad_in = jnp.dot(normed, pre_grad, preferred_element_type=jnp.float32)
    hvp_in = jnp.dot(normed, pre_grad_dot, preferred_element_type=jnp.float32)
    new_mom_in, new_hess_in, step_in = sophia_update(mom_in, hess_in, grad_in, hvp_in, probe_in)
    new_mom_out, new_hess_out, step_out = sophia_update(mom_out, hess_out, grad_out, hvp_out, probe_out)
    return (new_mom_in, new_hess_in, step_in, new_mom_out, new_hess_out, step_out)
```

```python
import jax
import jax.numpy as jnp
from jax import lax
from jax.sharding import Mesh, PartitionSpec as P

D = 7168
FF = 14336


BETA_ONE = 0.96
BETA_TWO = 0.99
SCALE_GAMMA = 0.05
FLOOR_EPS = 0.002
NORM_EPS = 1e-05
hash_factor = 73244475
contract_rows = (((0,), (0,)), ((), ()))
contract_cols = (((1,), (1,)), ((), ()))
PLANE = ("y", "x")
DEPTH = ("h",)
DP = PLANE + DEPTH
TENSOR = ("l", "c")


def mixing(words):
    words = (words ^ words >> 16 & 65535) * hash_factor
    words = (words ^ words >> 16 & 65535) * hash_factor
    return words ^ words >> 16 & 65535


def probe_signs(seed_word, row_start, col_start, row_count, col_count, total_cols):
    rows_index = row_start + jnp.arange(row_count, dtype=jnp.int32)[:, None]
    cols_index = col_start + jnp.arange(col_count, dtype=jnp.int32)[None, :]
    hashed = mixing(rows_index * total_cols + cols_index ^ seed_word)
    return (1 - 2 * (hashed & 1)).astype(jnp.bfloat16)


def gelu_parts(preact):
    normal_cdf = 0.5 * (1.0 + lax.erf(preact * 0.7071067811865476))
    normal_pdf = jnp.exp(-0.5 * preact * preact) * 0.3989422804014327
    return (
        preact * normal_cdf,
        normal_cdf + preact * normal_pdf,
        normal_pdf * (2.0 - preact * preact),
    )


def token_weights(segment_ids):
    following = jnp.concatenate([segment_ids[1:], jnp.full((1,), -1, jnp.int32)])
    valid = (following == segment_ids).astype(jnp.float32)
    same_doc = (segment_ids[:, None] == segment_ids[None, :]).astype(jnp.float32)
    counts = jnp.dot(same_doc, valid, precision=lax.Precision.HIGHEST)
    return valid / jnp.maximum(counts, 1.0)


def sophia_update(moment_old, curve_old, gradient, product, probe):
    moment = BETA_ONE * moment_old.astype(jnp.float32) + (1.0 - BETA_ONE) * gradient
    curvature = (
        BETA_TWO * curve_old.astype(jnp.float32)
        + (1.0 - BETA_TWO) * probe.astype(jnp.float32) * product
    )
    stepped = jnp.clip(moment / jnp.maximum(SCALE_GAMMA * curvature, FLOOR_EPS), -1.0, 1.0)
    return (
        moment.astype(jnp.bfloat16),
        curvature.astype(jnp.bfloat16),
        stepped.astype(jnp.bfloat16),
    )


def swap(blocks, axes):
    return lax.all_to_all(blocks, axes, 0, 0, tiled=True)


def spread(block, axes):
    count = lax.axis_size(axes)
    return swap(jnp.broadcast_to(block[None], (count,) + block.shape), axes)


def norm_stats(values):
    features = values.shape[0]
    own_mean = jnp.sum(values, axis=0) / features
    own_centered = values - own_mean
    own_square = jnp.sum(own_centered * own_centered, axis=0)
    every = spread(jnp.stack([own_mean, own_square]), DP)
    mean_val = jnp.mean(every[:, 0], axis=0)
    apart = every[:, 0] - mean_val
    variance = jnp.sum(every[:, 1] + features * apart * apart, axis=0) / D
    return mean_val, variance


def summed_block(first, second):
    width, tokens = first.shape
    planes = lax.axis_size(PLANE)
    blocks = jnp.concatenate(
        [part.astype(jnp.bfloat16).reshape(planes, width // planes, tokens) for part in (first, second)],
        axis=1,
    )
    own = jnp.sum(swap(blocks, PLANE).astype(jnp.float32), axis=0).astype(jnp.bfloat16)
    total = jnp.sum(spread(own, DEPTH).astype(jnp.float32), axis=0)
    return total[: width // planes], total[width // planes :]


def gathered_pair(first, second):
    units, tokens = first.shape
    both = spread(jnp.concatenate([first, second], axis=0).astype(jnp.bfloat16), PLANE)
    return both[:, :units].reshape(-1, tokens), both[:, units:].reshape(-1, tokens)


def body(inputs, ln_gain, segment_ids, w_in, w_out, mom_in, mom_out, hess_in, hess_out, probe_seed):
    features, length = inputs.shape
    hidden_width = w_in.shape[1]
    values = inputs.astype(jnp.float32)
    mean_val, variance = norm_stats(values)
    centered = values - mean_val
    normed = (centered * lax.rsqrt(variance + NORM_EPS) * ln_gain[:, None]).astype(jnp.bfloat16)
    row_start = lax.axis_index(DP) * features
    col_start = lax.axis_index(TENSOR) * hidden_width
    probe_in = probe_signs(probe_seed[0], row_start, col_start, features, hidden_width, FF)
    probe_out = probe_signs(probe_seed[1], row_start, col_start, features, hidden_width, FF)

    def onto_hidden(weight, block):
        return lax.dot_general(weight, block, contract_rows, preferred_element_type=jnp.float32)

    def onto_features(weight, block):
        return jnp.dot(weight, block, preferred_element_type=jnp.float32)

    def onto_weight(left, right):
        return lax.dot_general(left, right, contract_cols, preferred_element_type=jnp.float32)

    pre, pre_dot = summed_block(onto_hidden(w_in, normed), onto_hidden(probe_in, normed))
    act, slope, curve = gelu_parts(pre)
    hidden, hidden_dot = gathered_pair(act, slope * pre_dot)
    partial = jnp.stack(
        [
            onto_features(w_out, hidden),
            onto_features(w_out, hidden_dot) + onto_features(probe_out, hidden),
        ]
    ).astype(jnp.bfloat16)
    output, output_dot = jnp.sum(lax.all_gather(partial, TENSOR).astype(jnp.float32), axis=0)
    target = jnp.concatenate([values[:, 1:], jnp.zeros((features, 1), jnp.float32)], axis=1)
    weights = token_weights(segment_ids)
    cotangent = (weights * (output - target)).astype(jnp.bfloat16)
    cotangent_dot = (weights * output_dot).astype(jnp.bfloat16)
    back, back_dot = summed_block(
        onto_hidden(w_out, cotangent),
        onto_hidden(w_out, cotangent_dot) + onto_hidden(probe_out, cotangent),
    )
    pre_grad, pre_grad_dot = gathered_pair(
        slope * back, curve * pre_dot * back + slope * back_dot
    )
    grad_out = onto_weight(cotangent, hidden)
    hvp_out = onto_weight(cotangent_dot, hidden) + onto_weight(cotangent, hidden_dot)
    grad_in = onto_weight(normed, pre_grad)
    hvp_in = onto_weight(normed, pre_grad_dot)
    new_mom_in, new_hess_in, step_in = sophia_update(mom_in, hess_in, grad_in, hvp_in, probe_in)
    new_mom_out, new_hess_out, step_out = sophia_update(
        mom_out, hess_out, grad_out, hvp_out, probe_out
    )
    return (new_mom_in, new_hess_in, step_in, new_mom_out, new_hess_out, step_out)


def solution(mesh):
    torus = Mesh(mesh.devices.reshape(4, 4, 4, 2, 2), ("y", "x", "h", "l", "c"))
    matrix = P(DP, TENSOR)
    in_specs = (P(DP, None), P(DP), P()) + (matrix,) * 6 + (P(),)
    return jax.shard_map(
        body, mesh=torus, in_specs=in_specs, out_specs=(matrix,) * 6, check_vma=False
    )
```

```python
import jax
import jax.numpy as jnp
from jax import lax
from jax.sharding import Mesh, PartitionSpec as P

D = 7168
FF = 14336


BETA_ONE = 0.96
BETA_TWO = 0.99
SCALE_GAMMA = 0.05
FLOOR_EPS = 0.002
NORM_EPS = 1e-05
hash_factor = 73244475
contract_rows = (((0,), (0,)), ((), ()))
contract_cols = (((1,), (1,)), ((), ()))
PLANE = ("y", "x")
DEPTH = ("h",)
DP = PLANE + DEPTH
TENSOR = ("l", "c")


def mixing(words):
    words = (words ^ words >> 16 & 65535) * hash_factor
    words = (words ^ words >> 16 & 65535) * hash_factor
    return words ^ words >> 16 & 65535


def probe_signs(seed_word, rows_index, col_start, col_count):
    cols_index = col_start + jnp.arange(col_count, dtype=jnp.int32)[None, :]
    hashed = mixing(rows_index[:, None] * FF + cols_index ^ seed_word)
    return (1 - 2 * (hashed & 1)).astype(jnp.bfloat16)


def gelu_parts(preact):
    normal_cdf = 0.5 * (1.0 + lax.erf(preact * 0.7071067811865476))
    normal_pdf = jnp.exp(-0.5 * preact * preact) * 0.3989422804014327
    return (
        preact * normal_cdf,
        normal_cdf + preact * normal_pdf,
        normal_pdf * (2.0 - preact * preact),
    )


def token_weights(segment_ids):
    following = jnp.concatenate([segment_ids[1:], jnp.full((1,), -1, jnp.int32)])
    valid = (following == segment_ids).astype(jnp.float32)
    same_doc = (segment_ids[:, None] == segment_ids[None, :]).astype(jnp.float32)
    counts = jnp.dot(same_doc, valid, precision=lax.Precision.HIGHEST)
    return valid / jnp.maximum(counts, 1.0)


def sophia_update(moment_old, curve_old, gradient, product, probe):
    moment = BETA_ONE * moment_old.astype(jnp.float32) + (1.0 - BETA_ONE) * gradient
    curvature = (
        BETA_TWO * curve_old.astype(jnp.float32)
        + (1.0 - BETA_TWO) * probe.astype(jnp.float32) * product
    )
    stepped = jnp.clip(moment / jnp.maximum(SCALE_GAMMA * curvature, FLOOR_EPS), -1.0, 1.0)
    return (
        moment.astype(jnp.bfloat16),
        curvature.astype(jnp.bfloat16),
        stepped.astype(jnp.bfloat16),
    )


def swap(blocks, axes):
    return lax.all_to_all(blocks, axes, 0, 0, tiled=True)


def spread(block, axes):
    count = lax.axis_size(axes)
    return swap(jnp.broadcast_to(block[None], (count,) + block.shape), axes)


def turns(block):
    count = lax.axis_size(DEPTH)
    return [block] + [
        lax.ppermute(block, DEPTH, [(at, (at + shift) % count) for at in range(count)])
        for shift in range(1, count)
    ]


def three_terms(value):
    terms, rest = [], value
    for _ in range(3):
        terms.append(rest.astype(jnp.bfloat16))
        rest = rest - terms[-1].astype(jnp.float32)
    return terms


def column_blocks(matrix, count):
    rows, cols = matrix.shape
    return matrix.reshape(rows, count, cols // count).transpose(1, 0, 2)


def dot_rows(left, right, **options):
    return lax.dot_general(left, right, contract_rows, preferred_element_type=jnp.float32, **options)


def dot_cols(left, right):
    return lax.dot_general(left, right, contract_cols, preferred_element_type=jnp.float32)


def dot_plain(left, right):
    return jnp.dot(left, right, preferred_element_type=jnp.float32)


def body(inputs, ln_gain, segment_ids, w_in, w_out, mom_in, mom_out, hess_in, hess_out, probe_seed):
    features, length = inputs.shape
    hidden_width = w_in.shape[1]
    planes = lax.axis_size(PLANE)
    deep = lax.axis_size(DEPTH)
    units = hidden_width // planes
    plane_rows = planes * features
    padded = -(-units // length) * length
    values = inputs.astype(jnp.float32)

    row_index = lax.axis_index(DP) * features + jnp.arange(features, dtype=jnp.int32)
    col_start = lax.axis_index(TENSOR) * hidden_width
    plane_index = (
        (jnp.arange(planes, dtype=jnp.int32)[:, None] * deep + lax.axis_index(DEPTH)) * features
        + jnp.arange(features, dtype=jnp.int32)[None, :]
    ).reshape(plane_rows)
    unit_start = col_start + lax.axis_index(PLANE) * units

    gain_terms = jnp.stack(three_terms(ln_gain), axis=1)
    side = jnp.concatenate(
        [gain_terms, jnp.zeros((features, padded - units - 3), jnp.bfloat16), inputs], axis=1
    )
    sent = jnp.concatenate(
        [column_blocks(w_in, planes), jnp.broadcast_to(side[None], (planes,) + side.shape)], axis=2
    )
    got = swap(sent, PLANE).reshape(plane_rows, padded + length)
    plane_in = got[:, :units]
    gain_cols = got[:, units : units + 3]
    plane_gain = jnp.sum(gain_cols.astype(jnp.float32), axis=1, keepdims=True)
    plane_values = got[:, padded:].astype(jnp.float32)
    plane_out = swap(column_blocks(w_out, planes), PLANE).reshape(plane_rows, units)
    plane_probe_in = probe_signs(probe_seed[0], plane_index, unit_start, units)
    plane_probe_out = probe_signs(probe_seed[1], plane_index, unit_start, units)

    plane_mean = jnp.mean(plane_values, axis=0)
    plane_centered = plane_values - plane_mean
    plane_square = jnp.sum(plane_centered * plane_centered, axis=0)
    scaled = (plane_centered * plane_gain).astype(jnp.bfloat16)
    gain_sum = jnp.concatenate(
        [
            jnp.pad(jnp.sum(dot_rows(gain_cols, part), axis=0), (0, padded - units))
            for part in (plane_in, plane_probe_in)
        ]
    ).reshape(-1, length)
    extras = jnp.concatenate(
        [gain_sum.astype(jnp.bfloat16)]
        + [term[None] for term in three_terms(plane_mean) + three_terms(plane_square)],
        axis=0,
    )
    extra_rows = extras.shape[0]
    extras = jnp.pad(extras, ((0, -extra_rows % 16), (0, 0)))
    every = turns(
        jnp.concatenate(
            [
                dot_rows(plane_in, scaled).astype(jnp.bfloat16),
                dot_rows(plane_probe_in, scaled).astype(jnp.bfloat16),
                extras,
            ],
            axis=0,
        )
    )
    every = [part.astype(jnp.float32) for part in every]
    tails = jnp.stack([part[2 * units : 2 * units + extra_rows] for part in every])
    sums = tails[:, : 2 * padded // length].reshape(deep, 2, padded)[:, :, :units]
    stats = jnp.sum(tails[:, 2 * padded // length :].reshape(deep, 2, 3, length), axis=2)
    mean_val = jnp.mean(stats[:, 0], axis=0)
    apart = stats[:, 0] - mean_val
    variance = jnp.sum(stats[:, 1] + plane_rows * apart * apart, axis=0) / D
    scale = lax.rsqrt(variance + NORM_EPS)
    totals = sum(part[: 2 * units] for part in every)
    pre, pre_dot = (
        scale
        * (
            totals[at * units : (at + 1) * units]
            + dot_rows(sums[:, at], apart, precision=lax.Precision.HIGHEST)
        )
        for at in range(2)
    )

    act, slope, curve = gelu_parts(pre)
    hidden = act.astype(jnp.bfloat16)
    hidden_dot = (slope * pre_dot).astype(jnp.bfloat16)
    all_hidden = lax.all_gather(jnp.stack([hidden, hidden_dot]), PLANE, axis=1)
    all_hidden = all_hidden.reshape(2, hidden_width, length)

    parts = jnp.concatenate(
        [
            dot_plain(plane_out, hidden).astype(jnp.bfloat16).reshape(planes, features, length),
            (dot_plain(plane_out, hidden_dot) + dot_plain(plane_probe_out, hidden))
            .astype(jnp.bfloat16)
            .reshape(planes, features, length),
        ],
        axis=1,
    )
    share = jnp.sum(swap(parts, PLANE).astype(jnp.float32), axis=0).astype(jnp.bfloat16)
    share = share.reshape(2, features, length)
    output, output_dot = jnp.sum(lax.all_gather(share, TENSOR).astype(jnp.float32), axis=0)
    target = jnp.concatenate([values[:, 1:], jnp.zeros((features, 1), jnp.float32)], axis=1)
    weights = token_weights(segment_ids)
    cotangent = (weights * (output - target)).astype(jnp.bfloat16)
    cotangent_dot = (weights * output_dot).astype(jnp.bfloat16)

    plane_cot = spread(jnp.concatenate([cotangent, cotangent_dot], axis=0), PLANE)
    plane_cot_dot = plane_cot[:, features:].reshape(plane_rows, length)
    plane_cot = plane_cot[:, :features].reshape(plane_rows, length)
    back_parts = turns(
        jnp.concatenate(
            [
                dot_rows(plane_out, plane_cot),
                dot_rows(plane_out, plane_cot_dot) + dot_rows(plane_probe_out, plane_cot),
            ],
            axis=0,
        ).astype(jnp.bfloat16)
    )
    back_total = sum(part.astype(jnp.float32) for part in back_parts)
    back, back_dot = back_total[:units], back_total[units:]
    grads = spread(
        jnp.concatenate(
            [slope * back, curve * pre_dot * back + slope * back_dot], axis=0
        ).astype(jnp.bfloat16),
        PLANE,
    )
    pre_grad = grads[:, :units].reshape(hidden_width, length)
    pre_grad_dot = grads[:, units:].reshape(hidden_width, length)

    normed = ((values - mean_val) * scale * ln_gain[:, None]).astype(jnp.bfloat16)
    probe_in = probe_signs(probe_seed[0], row_index, col_start, hidden_width)
    probe_out = probe_signs(probe_seed[1], row_index, col_start, hidden_width)
    grad_out = dot_cols(cotangent, all_hidden[0])
    hvp_out = dot_cols(cotangent_dot, all_hidden[0]) + dot_cols(cotangent, all_hidden[1])
    grad_in = dot_cols(normed, pre_grad)
    hvp_in = dot_cols(normed, pre_grad_dot)
    new_mom_in, new_hess_in, step_in = sophia_update(mom_in, hess_in, grad_in, hvp_in, probe_in)
    new_mom_out, new_hess_out, step_out = sophia_update(
        mom_out, hess_out, grad_out, hvp_out, probe_out
    )
    return (new_mom_in, new_hess_in, step_in, new_mom_out, new_hess_out, step_out)


def solution(mesh):
    torus = Mesh(mesh.devices.reshape(4, 4, 4, 2, 2), ("y", "x", "h", "l", "c"))
    matrix = P(DP, TENSOR)
    in_specs = (P(DP, None), P(DP), P()) + (matrix,) * 6 + (P(),)
    return jax.shard_map(
        body, mesh=torus, in_specs=in_specs, out_specs=(matrix,) * 6, check_vma=False
    )
```

```python
import jax
import jax.numpy as jnp
from jax import lax
from jax.sharding import Mesh, PartitionSpec as P

D = 7168
FF = 14336


BETA_ONE = 0.96
BETA_TWO = 0.99
SCALE_GAMMA = 0.05
FLOOR_EPS = 0.002
NORM_EPS = 1e-05
hash_factor = 73244475
contract_rows = (((0,), (0,)), ((), ()))
contract_cols = (((1,), (1,)), ((), ()))
PLANE = ("y", "x")
DEPTH = ("h",)
DP = PLANE + DEPTH
TENSOR = ("l", "c")


def mixing(words):
    words = (words ^ words >> 16 & 65535) * hash_factor
    words = (words ^ words >> 16 & 65535) * hash_factor
    return words ^ words >> 16 & 65535


def probe_signs(seed_word, rows_index, col_start, col_count):
    cols_index = col_start + jnp.arange(col_count, dtype=jnp.int32)[None, :]
    hashed = mixing(rows_index[:, None] * FF + cols_index ^ seed_word)
    return (1 - 2 * (hashed & 1)).astype(jnp.bfloat16)


def gelu_parts(preact):
    normal_cdf = 0.5 * (1.0 + lax.erf(preact * 0.7071067811865476))
    normal_pdf = jnp.exp(-0.5 * preact * preact) * 0.3989422804014327
    return (
        preact * normal_cdf,
        normal_cdf + preact * normal_pdf,
        normal_pdf * (2.0 - preact * preact),
    )


def token_weights(segment_ids):
    following = jnp.concatenate([segment_ids[1:], jnp.full((1,), -1, jnp.int32)])
    valid = (following == segment_ids).astype(jnp.float32)
    same_doc = (segment_ids[:, None] == segment_ids[None, :]).astype(jnp.float32)
    counts = jnp.dot(same_doc, valid, precision=lax.Precision.HIGHEST)
    return valid / jnp.maximum(counts, 1.0)


def sophia_update(moment_old, curve_old, gradient, product, probe):
    moment = BETA_ONE * moment_old.astype(jnp.float32) + (1.0 - BETA_ONE) * gradient
    curvature = (
        BETA_TWO * curve_old.astype(jnp.float32)
        + (1.0 - BETA_TWO) * probe.astype(jnp.float32) * product
    )
    stepped = jnp.clip(moment / jnp.maximum(SCALE_GAMMA * curvature, FLOOR_EPS), -1.0, 1.0)
    return (
        moment.astype(jnp.bfloat16),
        curvature.astype(jnp.bfloat16),
        stepped.astype(jnp.bfloat16),
    )


def swap(blocks, axes):
    return lax.all_to_all(blocks, axes, 0, 0, tiled=True)


def spread(block, axes):
    count = lax.axis_size(axes)
    return swap(jnp.broadcast_to(block[None], (count,) + block.shape), axes)


def turns(block):
    count = lax.axis_size(DEPTH)
    return [block] + [
        lax.ppermute(block, DEPTH, [(at, (at + shift) % count) for at in range(count)])
        for shift in range(1, count)
    ]


def three_terms(value):
    terms, rest = [], value
    for _ in range(3):
        terms.append(rest.astype(jnp.bfloat16))
        rest = rest - terms[-1].astype(jnp.float32)
    return terms


def column_blocks(matrix, count):
    rows, cols = matrix.shape
    return matrix.reshape(rows, count, cols // count).transpose(1, 0, 2)


def dot_rows(left, right, **options):
    return lax.dot_general(left, right, contract_rows, preferred_element_type=jnp.float32, **options)


def dot_cols(left, right):
    return lax.dot_general(left, right, contract_cols, preferred_element_type=jnp.float32)


def dot_plain(left, right):
    return jnp.dot(left, right, preferred_element_type=jnp.float32)


def body(inputs, ln_gain, segment_ids, w_in, w_out, mom_in, mom_out, hess_in, hess_out, probe_seed):
    features, length = inputs.shape
    hidden_width = w_in.shape[1]
    planes = lax.axis_size(PLANE)
    deep = lax.axis_size(DEPTH)
    units = hidden_width // planes
    plane_rows = planes * features
    padded = -(-units // length) * length
    values = inputs.astype(jnp.float32)

    row_index = lax.axis_index(DP) * features + jnp.arange(features, dtype=jnp.int32)
    col_start = lax.axis_index(TENSOR) * hidden_width
    plane_index = (
        (jnp.arange(planes, dtype=jnp.int32)[:, None] * deep + lax.axis_index(DEPTH)) * features
        + jnp.arange(features, dtype=jnp.int32)[None, :]
    ).reshape(plane_rows)
    unit_start = col_start + lax.axis_index(PLANE) * units

    gain_terms = jnp.stack(three_terms(ln_gain), axis=1)
    side = jnp.concatenate(
        [gain_terms, jnp.zeros((features, padded - units - 3), jnp.bfloat16), inputs], axis=1
    )
    sent = jnp.concatenate(
        [column_blocks(w_in, planes), jnp.broadcast_to(side[None], (planes,) + side.shape)], axis=2
    )
    got = swap(sent, PLANE)
    out_blocks, got = lax.optimization_barrier((column_blocks(w_out, planes), got))
    plane_out = swap(out_blocks, PLANE).reshape(plane_rows, units)
    got = got.reshape(plane_rows, padded + length)
    plane_in = got[:, :units]
    gain_cols = got[:, units : units + 3]
    plane_gain = jnp.sum(gain_cols.astype(jnp.float32), axis=1, keepdims=True)
    plane_values = got[:, padded:].astype(jnp.float32)
    plane_probe_in = probe_signs(probe_seed[0], plane_index, unit_start, units)
    plane_probe_out = probe_signs(probe_seed[1], plane_index, unit_start, units)

    plane_mean = jnp.mean(plane_values, axis=0)
    plane_centered = plane_values - plane_mean
    plane_square = jnp.sum(plane_centered * plane_centered, axis=0)
    scaled = (plane_centered * plane_gain).astype(jnp.bfloat16)
    gain_sum = jnp.concatenate(
        [
            jnp.pad(jnp.sum(dot_rows(gain_cols, part), axis=0), (0, padded - units))
            for part in (plane_in, plane_probe_in)
        ]
    ).reshape(-1, length)
    extras = jnp.concatenate(
        [gain_sum.astype(jnp.bfloat16)]
        + [term[None] for term in three_terms(plane_mean) + three_terms(plane_square)],
        axis=0,
    )
    extra_rows = extras.shape[0]
    extras = jnp.pad(extras, ((0, -extra_rows % 16), (0, 0)))
    every = turns(
        jnp.concatenate(
            [
                dot_rows(plane_in, scaled).astype(jnp.bfloat16),
                dot_rows(plane_probe_in, scaled).astype(jnp.bfloat16),
                extras,
            ],
            axis=0,
        )
    )
    every, plane_out = lax.optimization_barrier((every, plane_out))
    every = [part.astype(jnp.float32) for part in every]
    tails = jnp.stack([part[2 * units : 2 * units + extra_rows] for part in every])
    sums = tails[:, : 2 * padded // length].reshape(deep, 2, padded)[:, :, :units]
    stats = jnp.sum(tails[:, 2 * padded // length :].reshape(deep, 2, 3, length), axis=2)
    mean_val = jnp.mean(stats[:, 0], axis=0)
    apart = stats[:, 0] - mean_val
    variance = jnp.sum(stats[:, 1] + plane_rows * apart * apart, axis=0) / D
    scale = lax.rsqrt(variance + NORM_EPS)
    totals = sum(part[: 2 * units] for part in every)
    pre, pre_dot = (
        scale
        * (
            totals[at * units : (at + 1) * units]
            + dot_rows(sums[:, at], apart, precision=lax.Precision.HIGHEST)
        )
        for at in range(2)
    )

    act, slope, curve = gelu_parts(pre)
    both = spread(jnp.concatenate([act, slope * pre_dot], axis=0).astype(jnp.bfloat16), PLANE)
    hidden = both[:, :units].reshape(hidden_width, length)
    hidden_dot = both[:, units:].reshape(hidden_width, length)

    probe_in = probe_signs(probe_seed[0], row_index, col_start, hidden_width)
    probe_out = probe_signs(probe_seed[1], row_index, col_start, hidden_width)
    share = jnp.stack(
        [
            dot_plain(w_out, hidden),
            dot_plain(w_out, hidden_dot) + dot_plain(probe_out, hidden),
        ]
    ).astype(jnp.bfloat16)
    output, output_dot = jnp.sum(lax.all_gather(share, TENSOR).astype(jnp.float32), axis=0)
    target = jnp.concatenate([values[:, 1:], jnp.zeros((features, 1), jnp.float32)], axis=1)
    weights = token_weights(segment_ids)
    cotangent = (weights * (output - target)).astype(jnp.bfloat16)
    cotangent_dot = (weights * output_dot).astype(jnp.bfloat16)

    plane_cot = spread(jnp.concatenate([cotangent, cotangent_dot], axis=0), PLANE)
    plane_cot_dot = plane_cot[:, features:].reshape(plane_rows, length)
    plane_cot = plane_cot[:, :features].reshape(plane_rows, length)
    back_parts = turns(
        jnp.concatenate(
            [
                dot_rows(plane_out, plane_cot),
                dot_rows(plane_out, plane_cot_dot) + dot_rows(plane_probe_out, plane_cot),
            ],
            axis=0,
        ).astype(jnp.bfloat16)
    )
    back_total = sum(part.astype(jnp.float32) for part in back_parts)
    back, back_dot = back_total[:units], back_total[units:]
    grads = spread(
        jnp.concatenate(
            [slope * back, curve * pre_dot * back + slope * back_dot], axis=0
        ).astype(jnp.bfloat16),
        PLANE,
    )
    pre_grad = grads[:, :units].reshape(hidden_width, length)
    pre_grad_dot = grads[:, units:].reshape(hidden_width, length)

    normed = ((values - mean_val) * scale * ln_gain[:, None]).astype(jnp.bfloat16)
    grad_out = dot_cols(cotangent, hidden)
    hvp_out = dot_cols(cotangent_dot, hidden) + dot_cols(cotangent, hidden_dot)
    grad_in = dot_cols(normed, pre_grad)
    hvp_in = dot_cols(normed, pre_grad_dot)
    new_mom_in, new_hess_in, step_in = sophia_update(mom_in, hess_in, grad_in, hvp_in, probe_in)
    new_mom_out, new_hess_out, step_out = sophia_update(
        mom_out, hess_out, grad_out, hvp_out, probe_out
    )
    return (new_mom_in, new_hess_in, step_in, new_mom_out, new_hess_out, step_out)


def solution(mesh):
    torus = Mesh(mesh.devices.reshape(4, 4, 4, 2, 2), ("y", "x", "h", "l", "c"))
    matrix = P(DP, TENSOR)
    in_specs = (P(DP, None), P(DP), P()) + (matrix,) * 6 + (P(),)
    return jax.shard_map(
        body, mesh=torus, in_specs=in_specs, out_specs=(matrix,) * 6, check_vma=False
    )
```

```python
import jax
import jax.numpy as jnp
from jax import lax
from jax.experimental import pallas as pl
from jax.experimental.pallas import tpu as pltpu
from jax.sharding import Mesh, PartitionSpec as P

D = 7168
FF = 14336


BETA_ONE = 0.96
BETA_TWO = 0.99
SCALE_GAMMA = 0.05
FLOOR_EPS = 0.002
NORM_EPS = 1e-05
hash_factor = 73244475
contract_rows = (((0,), (0,)), ((), ()))
contract_cols = (((1,), (1,)), ((), ()))
PLANE = ("y", "x")
DEPTH = ("h",)
DP = PLANE + DEPTH
TENSOR = ("l", "c")


def mixing(words):
    words = (words ^ words >> 16 & 65535) * hash_factor
    words = (words ^ words >> 16 & 65535) * hash_factor
    return words ^ words >> 16 & 65535


def probe_signs(seed_word, rows_index, col_start, col_count):
    cols_index = col_start + jnp.arange(col_count, dtype=jnp.int32)[None, :]
    hashed = mixing(rows_index[:, None] * FF + cols_index ^ seed_word)
    return (1 - 2 * (hashed & 1)).astype(jnp.bfloat16)


def gelu_parts(preact):
    normal_cdf = 0.5 * (1.0 + lax.erf(preact * 0.7071067811865476))
    normal_pdf = jnp.exp(-0.5 * preact * preact) * 0.3989422804014327
    return (
        preact * normal_cdf,
        normal_cdf + preact * normal_pdf,
        normal_pdf * (2.0 - preact * preact),
    )


def token_weights(segment_ids):
    following = jnp.concatenate([segment_ids[1:], jnp.full((1,), -1, jnp.int32)])
    valid = (following == segment_ids).astype(jnp.float32)
    same_doc = (segment_ids[:, None] == segment_ids[None, :]).astype(jnp.float32)
    counts = jnp.dot(same_doc, valid, precision=lax.Precision.HIGHEST)
    return valid / jnp.maximum(counts, 1.0)


def sophia_update(moment_old, curve_old, gradient, product, probe):
    moment = BETA_ONE * moment_old.astype(jnp.float32) + (1.0 - BETA_ONE) * gradient
    curvature = (
        BETA_TWO * curve_old.astype(jnp.float32)
        + (1.0 - BETA_TWO) * probe.astype(jnp.float32) * product
    )
    stepped = jnp.clip(moment / jnp.maximum(SCALE_GAMMA * curvature, FLOOR_EPS), -1.0, 1.0)
    return (
        moment.astype(jnp.bfloat16),
        curvature.astype(jnp.bfloat16),
        stepped.astype(jnp.bfloat16),
    )


def swap(blocks, axes):
    return lax.all_to_all(blocks, axes, 0, 0, tiled=True)


def spread(block, axes):
    count = lax.axis_size(axes)
    return swap(jnp.broadcast_to(block[None], (count,) + block.shape), axes)


def turns(block):
    count = lax.axis_size(DEPTH)
    return [block] + [
        lax.ppermute(block, DEPTH, [(at, (at + shift) % count) for at in range(count)])
        for shift in range(1, count)
    ]


def three_terms(value):
    terms, rest = [], value
    for _ in range(3):
        terms.append(rest.astype(jnp.bfloat16))
        rest = rest - terms[-1].astype(jnp.float32)
    return terms


def column_blocks(matrix, count):
    rows, cols = matrix.shape
    return matrix.reshape(rows, count, cols // count).transpose(1, 0, 2)


def pack_kernel(weight_ref, gain_ref, inputs_ref, sent_ref):
    count, rows, _ = sent_ref.shape
    units = weight_ref.shape[1] // count
    length = inputs_ref.shape[1]
    rest = units - length
    on_row = lax.broadcasted_iota(jnp.int32, (rows, rows), 0)
    on_col = lax.broadcasted_iota(jnp.int32, (rows, rows), 1)
    gain = jnp.sum(jnp.where(on_row == on_col, gain_ref[...], 0.0), axis=1, keepdims=True)
    lane = lax.broadcasted_iota(jnp.int32, (rows, length), 1)
    tail = jnp.zeros((rows, length), jnp.float32)
    for at, term in enumerate(three_terms(gain)):
        tail = jnp.where(lane == rest + at, term.astype(jnp.float32), tail)
    tail = tail[:, rest:].astype(jnp.bfloat16)
    for at in range(count):
        first = at * units
        sent_ref[at, :, 0:length] = weight_ref[:, first : first + length]
        sent_ref[at, :, length : 2 * length] = jnp.concatenate(
            [weight_ref[:, first + length : first + units], tail], axis=1
        )
        sent_ref[at, :, 2 * length : 3 * length] = inputs_ref[...]


def packed_blocks(weight, gain, inputs, count):
    rows, cols = weight.shape
    length = inputs.shape[1]
    group = 4
    return pl.pallas_call(
        pack_kernel,
        grid=(count // group,),
        in_specs=[
            pl.BlockSpec((rows, group * cols // count), lambda at: (0, at)),
            pl.BlockSpec((1, rows), lambda at: (0, 0)),
            pl.BlockSpec(inputs.shape, lambda at: (0, 0)),
        ],
        out_specs=pl.BlockSpec((group, rows, 3 * length), lambda at: (at, 0, 0)),
        out_shape=jax.ShapeDtypeStruct((count, rows, 3 * length), weight.dtype),
        cost_estimate=pl.CostEstimate(flops=0, bytes_accessed=5 * weight.size, transcendentals=0),
    )(weight, gain[None], inputs)


def dot_rows(left, right, **options):
    return lax.dot_general(left, right, contract_rows, preferred_element_type=jnp.float32, **options)


def dot_cols(left, right):
    return lax.dot_general(left, right, contract_cols, preferred_element_type=jnp.float32)


def dot_plain(left, right):
    return jnp.dot(left, right, preferred_element_type=jnp.float32)


def body(inputs, ln_gain, segment_ids, w_in, w_out, mom_in, mom_out, hess_in, hess_out, probe_seed):
    features, length = inputs.shape
    hidden_width = w_in.shape[1]
    planes = lax.axis_size(PLANE)
    deep = lax.axis_size(DEPTH)
    units = hidden_width // planes
    plane_rows = planes * features
    padded = -(-units // length) * length

    row_index = lax.axis_index(DP) * features + jnp.arange(features, dtype=jnp.int32)
    col_start = lax.axis_index(TENSOR) * hidden_width
    plane_index = (
        (jnp.arange(planes, dtype=jnp.int32)[:, None] * deep + lax.axis_index(DEPTH)) * features
        + jnp.arange(features, dtype=jnp.int32)[None, :]
    ).reshape(plane_rows)
    unit_start = col_start + lax.axis_index(PLANE) * units

    sent = packed_blocks(w_in, ln_gain, inputs, planes)
    sent, seeds, inputs, segment_ids = lax.optimization_barrier(
        (sent, probe_seed, inputs, segment_ids)
    )
    values = inputs.astype(jnp.float32)
    probes = (
        probe_signs(seeds[0], plane_index, unit_start, units),
        probe_signs(seeds[1], plane_index, unit_start, units),
        probe_signs(seeds[0], row_index, col_start, hidden_width),
        probe_signs(seeds[1], row_index, col_start, hidden_width),
    )
    target = jnp.concatenate([values[:, 1:], jnp.zeros((features, 1), jnp.float32)], axis=1)
    weights = token_weights(segment_ids)
    got, out_blocks, probes, target, weights = lax.optimization_barrier(
        (swap(sent, PLANE), column_blocks(w_out, planes), probes, target, weights)
    )
    plane_probe_in, plane_probe_out, probe_in, probe_out = probes
    got = got.reshape(plane_rows, padded + length)
    plane_in = got[:, :units]
    gain_cols = got[:, units : units + 3]
    plane_gain = jnp.sum(gain_cols.astype(jnp.float32), axis=1, keepdims=True)
    plane_values = got[:, padded:].astype(jnp.float32)

    plane_mean = jnp.mean(plane_values, axis=0)
    plane_centered = plane_values - plane_mean
    plane_square = jnp.sum(plane_centered * plane_centered, axis=0)
    scaled = (plane_centered * plane_gain).astype(jnp.bfloat16)
    gain_sum = jnp.concatenate(
        [
            jnp.pad(jnp.sum(dot_rows(gain_cols, part), axis=0), (0, padded - units))
            for part in (plane_in, plane_probe_in)
        ]
    ).reshape(-1, length)
    extras = jnp.concatenate(
        [gain_sum.astype(jnp.bfloat16)]
        + [term[None] for term in three_terms(plane_mean) + three_terms(plane_square)],
        axis=0,
    )
    extra_rows = extras.shape[0]
    extras = jnp.pad(extras, ((0, -extra_rows % 16), (0, 0)))
    own = jnp.concatenate(
        [
            dot_rows(plane_in, scaled).astype(jnp.bfloat16),
            dot_rows(plane_probe_in, scaled).astype(jnp.bfloat16),
            extras,
        ],
        axis=0,
    )
    own, out_blocks = lax.optimization_barrier((own, out_blocks))
    every, plane_out = lax.optimization_barrier((turns(own), swap(out_blocks, PLANE)))
    plane_out = plane_out.reshape(plane_rows, units)
    every = [part.astype(jnp.float32) for part in every]
    tails = jnp.stack([part[2 * units : 2 * units + extra_rows] for part in every])
    sums = tails[:, : 2 * padded // length].reshape(deep, 2, padded)[:, :, :units]
    stats = jnp.sum(tails[:, 2 * padded // length :].reshape(deep, 2, 3, length), axis=2)
    mean_val = jnp.mean(stats[:, 0], axis=0)
    apart = stats[:, 0] - mean_val
    variance = jnp.sum(stats[:, 1] + plane_rows * apart * apart, axis=0) / D
    scale = lax.rsqrt(variance + NORM_EPS)
    totals = sum(part[: 2 * units] for part in every)
    pre, pre_dot = (
        scale
        * (
            totals[at * units : (at + 1) * units]
            + dot_rows(sums[:, at], apart, precision=lax.Precision.HIGHEST)
        )
        for at in range(2)
    )

    act, slope, curve = gelu_parts(pre)
    both = spread(jnp.concatenate([act, slope * pre_dot], axis=0).astype(jnp.bfloat16), PLANE)
    hidden = both[:, :units].reshape(hidden_width, length)
    hidden_dot = both[:, units:].reshape(hidden_width, length)

    share = jnp.stack(
        [
            dot_plain(w_out, hidden),
            dot_plain(w_out, hidden_dot) + dot_plain(probe_out, hidden),
        ]
    ).astype(jnp.bfloat16)
    output, output_dot = jnp.sum(lax.all_gather(share, TENSOR).astype(jnp.float32), axis=0)
    cotangent = (weights * (output - target)).astype(jnp.bfloat16)
    cotangent_dot = (weights * output_dot).astype(jnp.bfloat16)

    plane_cot = spread(jnp.concatenate([cotangent, cotangent_dot], axis=0), PLANE)
    plane_cot_dot = plane_cot[:, features:].reshape(plane_rows, length)
    plane_cot = plane_cot[:, :features].reshape(plane_rows, length)
    own = jnp.concatenate(
        [
            dot_rows(plane_out, plane_cot),
            dot_rows(plane_out, plane_cot_dot) + dot_rows(plane_probe_out, plane_cot),
        ],
        axis=0,
    ).astype(jnp.bfloat16)
    own, cotangent, cotangent_dot = lax.optimization_barrier((own, cotangent, cotangent_dot))
    grad_out = dot_cols(cotangent, hidden)
    hvp_out = dot_cols(cotangent_dot, hidden) + dot_cols(cotangent, hidden_dot)
    outs = sophia_update(mom_out, hess_out, grad_out, hvp_out, probe_out)
    back_parts, outs = lax.optimization_barrier((turns(own), outs))
    back_total = sum(part.astype(jnp.float32) for part in back_parts)
    back, back_dot = back_total[:units], back_total[units:]
    grads = spread(
        jnp.concatenate(
            [slope * back, curve * pre_dot * back + slope * back_dot], axis=0
        ).astype(jnp.bfloat16),
        PLANE,
    )
    pre_grad = grads[:, :units].reshape(hidden_width, length)
    pre_grad_dot = grads[:, units:].reshape(hidden_width, length)

    normed = ((values - mean_val) * scale * ln_gain[:, None]).astype(jnp.bfloat16)
    grad_in = dot_cols(normed, pre_grad)
    hvp_in = dot_cols(normed, pre_grad_dot)
    new_mom_in, new_hess_in, step_in = sophia_update(mom_in, hess_in, grad_in, hvp_in, probe_in)
    return (new_mom_in, new_hess_in, step_in) + tuple(outs)


def solution(mesh):
    torus = Mesh(mesh.devices.reshape(4, 4, 4, 2, 2), ("y", "x", "h", "l", "c"))
    matrix = P(DP, TENSOR)
    in_specs = (P(DP, None), P(DP), P()) + (matrix,) * 6 + (P(),)
    return jax.shard_map(
        body, mesh=torus, in_specs=in_specs, out_specs=(matrix,) * 6, check_vma=False
    )
```

```python
import jax
import jax.numpy as jnp
from jax import lax
from jax.experimental import pallas as pl
from jax.experimental.pallas import tpu as pltpu
from jax.sharding import Mesh, PartitionSpec as P

D = 7168
FF = 14336


BETA_ONE = 0.96
BETA_TWO = 0.99
SCALE_GAMMA = 0.05
FLOOR_EPS = 0.002
NORM_EPS = 1e-05
hash_factor = 73244475
contract_rows = (((0,), (0,)), ((), ()))
contract_cols = (((1,), (1,)), ((), ()))
PLANE = ("y", "x")
DEPTH = ("h",)
DP = PLANE + DEPTH
TENSOR = ("l", "c")
CORE = "c"


def mixing(words):
    words = (words ^ words >> 16 & 65535) * hash_factor
    words = (words ^ words >> 16 & 65535) * hash_factor
    return words ^ words >> 16 & 65535


def probe_signs(seed_word, rows_index, col_start, col_count):
    cols_index = col_start + jnp.arange(col_count, dtype=jnp.int32)[None, :]
    hashed = mixing(rows_index[:, None] * FF + cols_index ^ seed_word)
    return (1 - 2 * (hashed & 1)).astype(jnp.bfloat16)


def gelu_parts(preact):
    normal_cdf = 0.5 * (1.0 + lax.erf(preact * 0.7071067811865476))
    normal_pdf = jnp.exp(-0.5 * preact * preact) * 0.3989422804014327
    return (
        preact * normal_cdf,
        normal_cdf + preact * normal_pdf,
        normal_pdf * (2.0 - preact * preact),
    )


def token_weights(segment_ids):
    following = jnp.concatenate([segment_ids[1:], jnp.full((1,), -1, jnp.int32)])
    valid = (following == segment_ids).astype(jnp.float32)
    same_doc = (segment_ids[:, None] == segment_ids[None, :]).astype(jnp.float32)
    counts = jnp.dot(same_doc, valid, precision=lax.Precision.HIGHEST)
    return valid / jnp.maximum(counts, 1.0)


def sophia_update(moment_old, curve_old, gradient, product, probe):
    moment = BETA_ONE * moment_old.astype(jnp.float32) + (1.0 - BETA_ONE) * gradient
    curvature = (
        BETA_TWO * curve_old.astype(jnp.float32)
        + (1.0 - BETA_TWO) * probe.astype(jnp.float32) * product
    )
    stepped = jnp.clip(moment / jnp.maximum(SCALE_GAMMA * curvature, FLOOR_EPS), -1.0, 1.0)
    return (
        moment.astype(jnp.bfloat16),
        curvature.astype(jnp.bfloat16),
        stepped.astype(jnp.bfloat16),
    )


def swap(blocks, axes):
    return lax.all_to_all(blocks, axes, 0, 0, tiled=True)


def spread(block, axes):
    count = lax.axis_size(axes)
    return swap(jnp.broadcast_to(block[None], (count,) + block.shape), axes)


def turns(block):
    count = lax.axis_size(DEPTH)
    return [block] + [
        lax.ppermute(block, DEPTH, [(at, (at + shift) % count) for at in range(count)])
        for shift in range(1, count)
    ]


def three_terms(value):
    terms, rest = [], value
    for _ in range(3):
        terms.append(rest.astype(jnp.bfloat16))
        rest = rest - terms[-1].astype(jnp.float32)
    return terms


def pack_kernel(weight_ref, gain_ref, inputs_ref, sent_ref):
    count, rows, _ = sent_ref.shape
    units = weight_ref.shape[1] // count
    length = inputs_ref.shape[1]
    rest = units - length
    on_row = lax.broadcasted_iota(jnp.int32, (rows, rows), 0)
    on_col = lax.broadcasted_iota(jnp.int32, (rows, rows), 1)
    gain = jnp.sum(jnp.where(on_row == on_col, gain_ref[...], 0.0), axis=1, keepdims=True)
    lane = lax.broadcasted_iota(jnp.int32, (rows, length), 1)
    tail = jnp.zeros((rows, length), jnp.float32)
    for at, term in enumerate(three_terms(gain)):
        tail = jnp.where(lane == rest + at, term.astype(jnp.float32), tail)
    tail = tail[:, rest:].astype(jnp.bfloat16)
    for at in range(count):
        first = at * units
        sent_ref[at, :, 0:length] = weight_ref[:, first : first + length]
        sent_ref[at, :, length : 2 * length] = jnp.concatenate(
            [weight_ref[:, first + length : first + units], tail], axis=1
        )
        sent_ref[at, :, 2 * length : 3 * length] = inputs_ref[...]


def packed_blocks(weight, gain, inputs, count):
    rows, cols = weight.shape
    length = inputs.shape[1]
    group = 4
    return pl.pallas_call(
        pack_kernel,
        grid=(count // group,),
        in_specs=[
            pl.BlockSpec((rows, group * cols // count), lambda at: (0, at)),
            pl.BlockSpec((1, rows), lambda at: (0, 0)),
            pl.BlockSpec(inputs.shape, lambda at: (0, 0)),
        ],
        out_specs=pl.BlockSpec((group, rows, 3 * length), lambda at: (at, 0, 0)),
        out_shape=jax.ShapeDtypeStruct((count, rows, 3 * length), weight.dtype),
        cost_estimate=pl.CostEstimate(flops=0, bytes_accessed=5 * weight.size, transcendentals=0),
    )(weight, gain[None], inputs)


def column_kernel(weight_ref, blocks_ref):
    count, rows, padded = blocks_ref.shape
    units = weight_ref.shape[1] // count
    for at in range(count):
        blocks_ref[at] = jnp.concatenate(
            [
                weight_ref[:, at * units : (at + 1) * units],
                jnp.zeros((rows, padded - units), weight_ref.dtype),
            ],
            axis=1,
        )


def column_blocks(weight, count, lanes):
    rows, cols = weight.shape
    padded = -(-cols // count // lanes) * lanes
    group = 4
    return pl.pallas_call(
        column_kernel,
        grid=(count // group,),
        in_specs=[pl.BlockSpec((rows, group * cols // count), lambda at: (0, at))],
        out_specs=pl.BlockSpec((group, rows, padded), lambda at: (at, 0, 0)),
        out_shape=jax.ShapeDtypeStruct((count, rows, padded), weight.dtype),
        cost_estimate=pl.CostEstimate(flops=0, bytes_accessed=5 * weight.size, transcendentals=0),
    )(weight)


def dot_rows(left, right, **options):
    return lax.dot_general(left, right, contract_rows, preferred_element_type=jnp.float32, **options)


def dot_cols(left, right):
    return lax.dot_general(left, right, contract_cols, preferred_element_type=jnp.float32)


def dot_plain(left, right):
    return jnp.dot(left, right, preferred_element_type=jnp.float32)


def body(inputs, ln_gain, segment_ids, w_in, w_out, mom_in, mom_out, hess_in, hess_out, probe_seed):
    features, length = inputs.shape
    hidden_width = w_in.shape[1]
    planes = lax.axis_size(PLANE)
    deep = lax.axis_size(DEPTH)
    units = hidden_width // planes
    plane_rows = planes * features
    padded = -(-units // length) * length

    row_index = lax.axis_index(DP) * features + jnp.arange(features, dtype=jnp.int32)
    col_start = lax.axis_index(TENSOR) * hidden_width
    plane_index = (
        (jnp.arange(planes, dtype=jnp.int32)[:, None] * deep + lax.axis_index(DEPTH)) * features
        + jnp.arange(features, dtype=jnp.int32)[None, :]
    ).reshape(plane_rows)
    unit_start = col_start + lax.axis_index(PLANE) * units

    sent = packed_blocks(w_in, ln_gain, inputs, planes)
    sent, seeds, inputs, segment_ids, later_out = lax.optimization_barrier(
        (sent, probe_seed, inputs, segment_ids, w_out)
    )
    values = inputs.astype(jnp.float32)
    probes = (
        probe_signs(seeds[0], plane_index, unit_start, units),
        probe_signs(seeds[1], plane_index, unit_start, units),
        probe_signs(seeds[0], row_index, col_start, hidden_width),
        probe_signs(seeds[1], row_index, col_start, hidden_width),
    )
    target = jnp.concatenate([values[:, 1:], jnp.zeros((features, 1), jnp.float32)], axis=1)
    weights = token_weights(segment_ids)
    first_core = lax.axis_index(CORE) == 0
    got, out_blocks, probes, target, weights, first_core = lax.optimization_barrier(
        (swap(sent, PLANE), column_blocks(later_out, planes, length), probes, target, weights, first_core)
    )
    plane_probe_in, plane_probe_out, probe_in, probe_out = probes
    got = got.reshape(plane_rows, padded + length)
    plane_in = got[:, :units]
    gain_cols = got[:, units : units + 3]
    plane_gain = jnp.sum(gain_cols.astype(jnp.float32), axis=1, keepdims=True)
    plane_values = got[:, padded:].astype(jnp.float32)

    plane_mean = jnp.mean(plane_values, axis=0)
    plane_centered = plane_values - plane_mean
    plane_square = jnp.sum(plane_centered * plane_centered, axis=0)
    scaled = (plane_centered * plane_gain).astype(jnp.bfloat16)
    gain_sum = jnp.concatenate(
        [
            jnp.pad(jnp.sum(dot_rows(gain_cols, part), axis=0), (0, padded - units))
            for part in (plane_in, plane_probe_in)
        ]
    ).reshape(-1, length)
    extras = jnp.concatenate(
        [gain_sum.astype(jnp.bfloat16)]
        + [term[None] for term in three_terms(plane_mean) + three_terms(plane_square)],
        axis=0,
    )
    extra_rows = extras.shape[0]
    extras = jnp.pad(extras, ((0, -extra_rows % 16), (0, 0)))
    own = jnp.concatenate(
        [
            dot_rows(plane_in, scaled).astype(jnp.bfloat16),
            dot_rows(plane_probe_in, scaled).astype(jnp.bfloat16),
            extras,
        ],
        axis=0,
    )
    own, out_blocks = lax.optimization_barrier((own, out_blocks))
    every, plane_out = lax.optimization_barrier((turns(own), swap(out_blocks, PLANE)))
    plane_out = plane_out.reshape(plane_rows, padded)[:, :units]
    every = [part.astype(jnp.float32) for part in every]
    tails = jnp.stack([part[2 * units : 2 * units + extra_rows] for part in every])
    sums = tails[:, : 2 * padded // length].reshape(deep, 2, padded)[:, :, :units]
    stats = jnp.sum(tails[:, 2 * padded // length :].reshape(deep, 2, 3, length), axis=2)
    mean_val = jnp.mean(stats[:, 0], axis=0)
    apart = stats[:, 0] - mean_val
    variance = jnp.sum(stats[:, 1] + plane_rows * apart * apart, axis=0) / D
    scale = lax.rsqrt(variance + NORM_EPS)
    totals = sum(part[: 2 * units] for part in every)
    pre, pre_dot = (
        scale
        * (
            totals[at * units : (at + 1) * units]
            + dot_rows(sums[:, at], apart, precision=lax.Precision.HIGHEST)
        )
        for at in range(2)
    )

    act, slope, curve = gelu_parts(pre)
    both = spread(jnp.concatenate([act, slope * pre_dot], axis=0).astype(jnp.bfloat16), PLANE)
    hidden = both[:, :units].reshape(hidden_width, length)
    hidden_dot = both[:, units:].reshape(hidden_width, length)

    share = jnp.stack(
        [
            dot_plain(w_out, hidden),
            dot_plain(w_out, hidden_dot) + dot_plain(probe_out, hidden),
        ]
    ).astype(jnp.bfloat16)
    output, output_dot = jnp.sum(lax.all_gather(share, TENSOR).astype(jnp.float32), axis=0)
    cotangent = (weights * (output - target)).astype(jnp.bfloat16)
    cotangent_dot = (weights * output_dot).astype(jnp.bfloat16)

    held = spread(jnp.where(first_core, cotangent, cotangent_dot), PLANE).reshape(plane_rows, length)
    other = lax.ppermute(held, CORE, [(0, 1), (1, 0)])
    plane_cot = jnp.where(first_core, held, other)
    plane_cot_dot = jnp.where(first_core, other, held)
    own = jnp.concatenate(
        [
            dot_rows(plane_out, plane_cot),
            dot_rows(plane_out, plane_cot_dot) + dot_rows(plane_probe_out, plane_cot),
        ],
        axis=0,
    ).astype(jnp.bfloat16)
    own, cotangent, cotangent_dot = lax.optimization_barrier((own, cotangent, cotangent_dot))
    grad_out = dot_cols(cotangent, hidden)
    hvp_out = dot_cols(cotangent_dot, hidden) + dot_cols(cotangent, hidden_dot)
    outs = sophia_update(mom_out, hess_out, grad_out, hvp_out, probe_out)
    back_parts, outs = lax.optimization_barrier((turns(own), outs))
    back_total = sum(part.astype(jnp.float32) for part in back_parts)
    back, back_dot = back_total[:units], back_total[units:]
    grads = spread(
        jnp.concatenate(
            [slope * back, curve * pre_dot * back + slope * back_dot], axis=0
        ).astype(jnp.bfloat16),
        PLANE,
    )
    pre_grad = grads[:, :units].reshape(hidden_width, length)
    pre_grad_dot = grads[:, units:].reshape(hidden_width, length)

    normed = ((values - mean_val) * scale * ln_gain[:, None]).astype(jnp.bfloat16)
    grad_in = dot_cols(normed, pre_grad)
    hvp_in = dot_cols(normed, pre_grad_dot)
    new_mom_in, new_hess_in, step_in = sophia_update(mom_in, hess_in, grad_in, hvp_in, probe_in)
    return (new_mom_in, new_hess_in, step_in) + tuple(outs)


def solution(mesh):
    torus = Mesh(mesh.devices.reshape(4, 4, 4, 2, 2), ("y", "x", "h", "l", "c"))
    matrix = P(DP, TENSOR)
    in_specs = (P(DP, None), P(DP), P()) + (matrix,) * 6 + (P(),)
    return jax.shard_map(
        body, mesh=torus, in_specs=in_specs, out_specs=(matrix,) * 6, check_vma=False
    )
```

```python
import jax
import jax.numpy as jnp
from jax import lax
from jax.experimental import pallas as pl
from jax.experimental.pallas import tpu as pltpu
from jax.sharding import Mesh, PartitionSpec as P

D = 7168
FF = 14336


BETA_ONE = 0.96
BETA_TWO = 0.99
SCALE_GAMMA = 0.05
FLOOR_EPS = 0.002
NORM_EPS = 1e-05
hash_factor = 73244475
contract_rows = (((0,), (0,)), ((), ()))
contract_cols = (((1,), (1,)), ((), ()))
PLANE = ("y", "x")
DEPTH = ("h",)
DP = PLANE + DEPTH
TENSOR = ("l", "c")
CORE = "c"


def mixing(words):
    words = (words ^ words >> 16 & 65535) * hash_factor
    words = (words ^ words >> 16 & 65535) * hash_factor
    return words ^ words >> 16 & 65535


def probe_signs(seed_word, rows_index, col_start, col_count):
    cols_index = col_start + jnp.arange(col_count, dtype=jnp.int32)[None, :]
    hashed = mixing(rows_index[:, None] * FF + cols_index ^ seed_word)
    return (1 - 2 * (hashed & 1)).astype(jnp.bfloat16)


def gelu_parts(preact):
    normal_cdf = 0.5 * (1.0 + lax.erf(preact * 0.7071067811865476))
    normal_pdf = jnp.exp(-0.5 * preact * preact) * 0.3989422804014327
    return (
        preact * normal_cdf,
        normal_cdf + preact * normal_pdf,
        normal_pdf * (2.0 - preact * preact),
    )


def token_weights(segment_ids):
    following = jnp.concatenate([segment_ids[1:], jnp.full((1,), -1, jnp.int32)])
    valid = (following == segment_ids).astype(jnp.float32)
    same_doc = (segment_ids[:, None] == segment_ids[None, :]).astype(jnp.float32)
    counts = jnp.dot(same_doc, valid, precision=lax.Precision.HIGHEST)
    return valid / jnp.maximum(counts, 1.0)


def sophia_update(moment_old, curve_old, gradient, product, probe):
    moment = BETA_ONE * moment_old.astype(jnp.float32) + (1.0 - BETA_ONE) * gradient
    curvature = (
        BETA_TWO * curve_old.astype(jnp.float32)
        + (1.0 - BETA_TWO) * probe.astype(jnp.float32) * product
    )
    stepped = jnp.clip(moment / jnp.maximum(SCALE_GAMMA * curvature, FLOOR_EPS), -1.0, 1.0)
    return (
        moment.astype(jnp.bfloat16),
        curvature.astype(jnp.bfloat16),
        stepped.astype(jnp.bfloat16),
    )


def update_kernel(normed_ref, grads_ref, probe_ref, mom_ref, hess_ref, new_mom, new_hess, step):
    count, both, _ = grads_ref.shape
    units = both // 2
    normed = normed_ref[...]
    pre_grad = jnp.concatenate([grads_ref[at, 0:units] for at in range(count)], axis=0)
    pre_grad_dot = jnp.concatenate([grads_ref[at, units:both] for at in range(count)], axis=0)
    new_mom[...], new_hess[...], step[...] = sophia_update(
        mom_ref[...],
        hess_ref[...],
        dot_cols(normed, pre_grad),
        dot_cols(normed, pre_grad_dot),
        probe_ref[...],
    )


def updated(normed, grads, probe, mom, hess):
    count, both, length = grads.shape
    rows, cols = mom.shape
    group = 4
    wide = pl.BlockSpec((rows, group * cols // count), lambda at: (0, at))
    return pl.pallas_call(
        update_kernel,
        grid=(count // group,),
        in_specs=[
            pl.BlockSpec(normed.shape, lambda at: (0, 0)),
            pl.BlockSpec((group, both, length), lambda at: (at, 0, 0)),
            wide,
            wide,
            wide,
        ],
        out_specs=[wide] * 3,
        out_shape=[jax.ShapeDtypeStruct(mom.shape, mom.dtype)] * 3,
        cost_estimate=pl.CostEstimate(
            flops=4 * rows * cols * length, bytes_accessed=16 * mom.size, transcendentals=0
        ),
        compiler_params=pltpu.CompilerParams(vmem_limit_bytes=32 * 1024 * 1024),
    )(normed, grads, probe, mom, hess)


def swap(blocks, axes):
    return lax.all_to_all(blocks, axes, 0, 0, tiled=True)


def spread(block, axes):
    count = lax.axis_size(axes)
    return swap(jnp.broadcast_to(block[None], (count,) + block.shape), axes)


def turns(block):
    count = lax.axis_size(DEPTH)
    return [block] + [
        lax.ppermute(block, DEPTH, [(at, (at + shift) % count) for at in range(count)])
        for shift in range(1, count)
    ]


def three_terms(value):
    terms, rest = [], value
    for _ in range(3):
        terms.append(rest.astype(jnp.bfloat16))
        rest = rest - terms[-1].astype(jnp.float32)
    return terms


def pack_kernel(weight_ref, gain_ref, inputs_ref, sent_ref):
    count, rows, _ = sent_ref.shape
    units = weight_ref.shape[1] // count
    length = inputs_ref.shape[1]
    rest = units - length
    on_row = lax.broadcasted_iota(jnp.int32, (rows, rows), 0)
    on_col = lax.broadcasted_iota(jnp.int32, (rows, rows), 1)
    gain = jnp.sum(jnp.where(on_row == on_col, gain_ref[...], 0.0), axis=1, keepdims=True)
    lane = lax.broadcasted_iota(jnp.int32, (rows, length), 1)
    tail = jnp.zeros((rows, length), jnp.float32)
    for at, term in enumerate(three_terms(gain)):
        tail = jnp.where(lane == rest + at, term.astype(jnp.float32), tail)
    tail = tail[:, rest:].astype(jnp.bfloat16)
    for at in range(count):
        first = at * units
        sent_ref[at, :, 0:length] = weight_ref[:, first : first + length]
        sent_ref[at, :, length : 2 * length] = jnp.concatenate(
            [weight_ref[:, first + length : first + units], tail], axis=1
        )
        sent_ref[at, :, 2 * length : 3 * length] = inputs_ref[...]


def packed_blocks(weight, gain, inputs, count):
    rows, cols = weight.shape
    length = inputs.shape[1]
    group = 4
    return pl.pallas_call(
        pack_kernel,
        grid=(count // group,),
        in_specs=[
            pl.BlockSpec((rows, group * cols // count), lambda at: (0, at)),
            pl.BlockSpec((1, rows), lambda at: (0, 0)),
            pl.BlockSpec(inputs.shape, lambda at: (0, 0)),
        ],
        out_specs=pl.BlockSpec((group, rows, 3 * length), lambda at: (at, 0, 0)),
        out_shape=jax.ShapeDtypeStruct((count, rows, 3 * length), weight.dtype),
        cost_estimate=pl.CostEstimate(flops=0, bytes_accessed=5 * weight.size, transcendentals=0),
    )(weight, gain[None], inputs)


def column_kernel(weight_ref, blocks_ref):
    count, rows, padded = blocks_ref.shape
    units = weight_ref.shape[1] // count
    for at in range(count):
        blocks_ref[at] = jnp.concatenate(
            [
                weight_ref[:, at * units : (at + 1) * units],
                jnp.zeros((rows, padded - units), weight_ref.dtype),
            ],
            axis=1,
        )


def column_blocks(weight, count, lanes):
    rows, cols = weight.shape
    padded = -(-cols // count // lanes) * lanes
    group = 4
    return pl.pallas_call(
        column_kernel,
        grid=(count // group,),
        in_specs=[pl.BlockSpec((rows, group * cols // count), lambda at: (0, at))],
        out_specs=pl.BlockSpec((group, rows, padded), lambda at: (at, 0, 0)),
        out_shape=jax.ShapeDtypeStruct((count, rows, padded), weight.dtype),
        cost_estimate=pl.CostEstimate(flops=0, bytes_accessed=5 * weight.size, transcendentals=0),
    )(weight)


def dot_rows(left, right, **options):
    return lax.dot_general(left, right, contract_rows, preferred_element_type=jnp.float32, **options)


def dot_cols(left, right):
    return lax.dot_general(left, right, contract_cols, preferred_element_type=jnp.float32)


def dot_plain(left, right):
    return jnp.dot(left, right, preferred_element_type=jnp.float32)


def body(inputs, ln_gain, segment_ids, w_in, w_out, mom_in, mom_out, hess_in, hess_out, probe_seed):
    features, length = inputs.shape
    hidden_width = w_in.shape[1]
    planes = lax.axis_size(PLANE)
    deep = lax.axis_size(DEPTH)
    units = hidden_width // planes
    plane_rows = planes * features
    padded = -(-units // length) * length

    row_index = lax.axis_index(DP) * features + jnp.arange(features, dtype=jnp.int32)
    col_start = lax.axis_index(TENSOR) * hidden_width
    plane_index = (
        (jnp.arange(planes, dtype=jnp.int32)[:, None] * deep + lax.axis_index(DEPTH)) * features
        + jnp.arange(features, dtype=jnp.int32)[None, :]
    ).reshape(plane_rows)
    unit_start = col_start + lax.axis_index(PLANE) * units

    sent = packed_blocks(w_in, ln_gain, inputs, planes)
    sent, seeds, inputs, segment_ids, later_out = lax.optimization_barrier(
        (sent, probe_seed, inputs, segment_ids, w_out)
    )
    values = inputs.astype(jnp.float32)
    probes = (
        probe_signs(seeds[0], plane_index, unit_start, units),
        probe_signs(seeds[1], plane_index, unit_start, units),
        probe_signs(seeds[0], row_index, col_start, hidden_width),
        probe_signs(seeds[1], row_index, col_start, hidden_width),
    )
    target = jnp.concatenate([values[:, 1:], jnp.zeros((features, 1), jnp.float32)], axis=1)
    weights = token_weights(segment_ids)
    first_core = lax.axis_index(CORE) == 0
    got, out_blocks, probes, target, weights, first_core = lax.optimization_barrier(
        (swap(sent, PLANE), column_blocks(later_out, planes, length), probes, target, weights, first_core)
    )
    plane_probe_in, plane_probe_out, probe_in, probe_out = probes
    got = got.reshape(plane_rows, padded + length)
    plane_in = got[:, :units]
    gain_cols = got[:, units : units + 3]
    plane_gain = jnp.sum(gain_cols.astype(jnp.float32), axis=1, keepdims=True)
    plane_values = got[:, padded:].astype(jnp.float32)

    plane_mean = jnp.mean(plane_values, axis=0)
    plane_centered = plane_values - plane_mean
    plane_square = jnp.sum(plane_centered * plane_centered, axis=0)
    scaled = (plane_centered * plane_gain).astype(jnp.bfloat16)
    gain_sum = jnp.concatenate(
        [
            jnp.pad(jnp.sum(dot_rows(gain_cols, part), axis=0), (0, padded - units))
            for part in (plane_in, plane_probe_in)
        ]
    ).reshape(-1, length)
    extras = jnp.concatenate(
        [gain_sum.astype(jnp.bfloat16)]
        + [term[None] for term in three_terms(plane_mean) + three_terms(plane_square)],
        axis=0,
    )
    extra_rows = extras.shape[0]
    extras = jnp.pad(extras, ((0, -extra_rows % 16), (0, 0)))
    own = jnp.concatenate(
        [
            dot_rows(plane_in, scaled).astype(jnp.bfloat16),
            dot_rows(plane_probe_in, scaled).astype(jnp.bfloat16),
            extras,
        ],
        axis=0,
    )
    own, out_blocks = lax.optimization_barrier((own, out_blocks))
    every, plane_out = lax.optimization_barrier((turns(own), swap(out_blocks, PLANE)))
    plane_out = plane_out.reshape(plane_rows, padded)[:, :units]
    every = [part.astype(jnp.float32) for part in every]
    tails = jnp.stack([part[2 * units : 2 * units + extra_rows] for part in every])
    sums = tails[:, : 2 * padded // length].reshape(deep, 2, padded)[:, :, :units]
    stats = jnp.sum(tails[:, 2 * padded // length :].reshape(deep, 2, 3, length), axis=2)
    mean_val = jnp.mean(stats[:, 0], axis=0)
    apart = stats[:, 0] - mean_val
    variance = jnp.sum(stats[:, 1] + plane_rows * apart * apart, axis=0) / D
    scale = lax.rsqrt(variance + NORM_EPS)
    totals = sum(part[: 2 * units] for part in every)
    pre, pre_dot = (
        scale
        * (
            totals[at * units : (at + 1) * units]
            + dot_rows(sums[:, at], apart, precision=lax.Precision.HIGHEST)
        )
        for at in range(2)
    )

    act, slope, curve = gelu_parts(pre)
    both = spread(jnp.concatenate([act, slope * pre_dot], axis=0).astype(jnp.bfloat16), PLANE)
    hidden = both[:, :units].reshape(hidden_width, length)
    hidden_dot = both[:, units:].reshape(hidden_width, length)

    share = jnp.stack(
        [
            dot_plain(w_out, hidden),
            dot_plain(w_out, hidden_dot) + dot_plain(probe_out, hidden),
        ]
    ).astype(jnp.bfloat16)
    output, output_dot = jnp.sum(lax.all_gather(share, TENSOR).astype(jnp.float32), axis=0)
    cotangent = (weights * (output - target)).astype(jnp.bfloat16)
    cotangent_dot = (weights * output_dot).astype(jnp.bfloat16)

    held = spread(jnp.where(first_core, cotangent, cotangent_dot), PLANE).reshape(plane_rows, length)
    other = lax.ppermute(held, CORE, [(0, 1), (1, 0)])
    plane_cot = jnp.where(first_core, held, other)
    plane_cot_dot = jnp.where(first_core, other, held)
    own = jnp.concatenate(
        [
            dot_rows(plane_out, plane_cot),
            dot_rows(plane_out, plane_cot_dot) + dot_rows(plane_probe_out, plane_cot),
        ],
        axis=0,
    ).astype(jnp.bfloat16)
    own, cotangent, cotangent_dot = lax.optimization_barrier((own, cotangent, cotangent_dot))
    grad_out = dot_cols(cotangent, hidden)
    hvp_out = dot_cols(cotangent_dot, hidden) + dot_cols(cotangent, hidden_dot)
    outs = sophia_update(mom_out, hess_out, grad_out, hvp_out, probe_out)
    normed = ((values - mean_val) * scale * ln_gain[:, None]).astype(jnp.bfloat16)
    back_parts, outs, normed = lax.optimization_barrier((turns(own), outs, normed))
    back_total = sum(part.astype(jnp.float32) for part in back_parts)
    back, back_dot = back_total[:units], back_total[units:]
    grads = spread(
        jnp.concatenate(
            [slope * back, curve * pre_dot * back + slope * back_dot], axis=0
        ).astype(jnp.bfloat16),
        PLANE,
    )

    new_mom_in, new_hess_in, step_in = updated(normed, grads, probe_in, mom_in, hess_in)
    return (new_mom_in, new_hess_in, step_in) + tuple(outs)


def solution(mesh):
    torus = Mesh(mesh.devices.reshape(4, 4, 4, 2, 2), ("y", "x", "h", "l", "c"))
    matrix = P(DP, TENSOR)
    in_specs = (P(DP, None), P(DP), P()) + (matrix,) * 6 + (P(),)
    return jax.shard_map(
        body, mesh=torus, in_specs=in_specs, out_specs=(matrix,) * 6, check_vma=False
    )
```

```python
import jax
import jax.numpy as jnp
from jax import lax
from jax.experimental import pallas as pl
from jax.experimental.pallas import tpu as pltpu
from jax.sharding import Mesh, PartitionSpec as P

D = 7168
FF = 14336


BETA_ONE = 0.96
BETA_TWO = 0.99
SCALE_GAMMA = 0.05
FLOOR_EPS = 0.002
NORM_EPS = 1e-05
hash_factor = 73244475
contract_rows = (((0,), (0,)), ((), ()))
contract_cols = (((1,), (1,)), ((), ()))
PLANE = ("y", "x")
DEPTH = ("h",)
DP = PLANE + DEPTH
TENSOR = ("l", "c")
CORE = "c"


def mixing(words):
    words = (words ^ words >> 16 & 65535) * hash_factor
    words = (words ^ words >> 16 & 65535) * hash_factor
    return words ^ words >> 16 & 65535


def probe_signs(seed_word, rows_index, col_start, col_count):
    cols_index = col_start + jnp.arange(col_count, dtype=jnp.int32)[None, :]
    hashed = mixing(rows_index[:, None] * FF + cols_index ^ seed_word)
    return (1 - 2 * (hashed & 1)).astype(jnp.bfloat16)


def gelu_parts(preact):
    normal_cdf = 0.5 * (1.0 + lax.erf(preact * 0.7071067811865476))
    normal_pdf = jnp.exp(-0.5 * preact * preact) * 0.3989422804014327
    return (
        preact * normal_cdf,
        normal_cdf + preact * normal_pdf,
        normal_pdf * (2.0 - preact * preact),
    )


def token_weights(segment_ids):
    following = jnp.concatenate([segment_ids[1:], jnp.full((1,), -1, jnp.int32)])
    valid = (following == segment_ids).astype(jnp.float32)
    same_doc = (segment_ids[:, None] == segment_ids[None, :]).astype(jnp.float32)
    counts = jnp.dot(same_doc, valid, precision=lax.Precision.HIGHEST)
    return valid / jnp.maximum(counts, 1.0)


def sophia_update(moment_old, curve_old, gradient, product, probe):
    moment = BETA_ONE * moment_old.astype(jnp.float32) + (1.0 - BETA_ONE) * gradient
    curvature = (
        BETA_TWO * curve_old.astype(jnp.float32)
        + (1.0 - BETA_TWO) * probe.astype(jnp.float32) * product
    )
    stepped = jnp.clip(moment / jnp.maximum(SCALE_GAMMA * curvature, FLOOR_EPS), -1.0, 1.0)
    return (
        moment.astype(jnp.bfloat16),
        curvature.astype(jnp.bfloat16),
        stepped.astype(jnp.bfloat16),
    )


def update_kernel(normed_ref, grads_ref, probe_ref, mom_ref, hess_ref, new_mom, new_hess, step):
    count, both, _ = grads_ref.shape
    units = both // 2
    normed = normed_ref[...]
    pre_grad = jnp.concatenate([grads_ref[at, 0:units] for at in range(count)], axis=0)
    pre_grad_dot = jnp.concatenate([grads_ref[at, units:both] for at in range(count)], axis=0)
    new_mom[...], new_hess[...], step[...] = sophia_update(
        mom_ref[...],
        hess_ref[...],
        dot_cols(normed, pre_grad),
        dot_cols(normed, pre_grad_dot),
        probe_ref[...],
    )


def updated(normed, grads, probe, mom, hess):
    count, both, length = grads.shape
    rows, cols = mom.shape
    group = 8
    wide = pl.BlockSpec((rows, group * cols // count), lambda at: (0, at))
    return pl.pallas_call(
        update_kernel,
        grid=(count // group,),
        in_specs=[
            pl.BlockSpec(normed.shape, lambda at: (0, 0)),
            pl.BlockSpec((group, both, length), lambda at: (at, 0, 0)),
            wide,
            wide,
            wide,
        ],
        out_specs=[wide] * 3,
        out_shape=[jax.ShapeDtypeStruct(mom.shape, mom.dtype)] * 3,
        cost_estimate=pl.CostEstimate(
            flops=4 * rows * cols * length, bytes_accessed=16 * mom.size, transcendentals=0
        ),
        compiler_params=pltpu.CompilerParams(vmem_limit_bytes=32 * 1024 * 1024),
    )(normed, grads, probe, mom, hess)


def swap(blocks, axes):
    return lax.all_to_all(blocks, axes, 0, 0, tiled=True)


def spread(block, axes):
    count = lax.axis_size(axes)
    return swap(jnp.broadcast_to(block[None], (count,) + block.shape), axes)


def turns(block):
    count = lax.axis_size(DEPTH)
    return [block] + [
        lax.ppermute(block, DEPTH, [(at, (at + shift) % count) for at in range(count)])
        for shift in range(1, count)
    ]


def three_terms(value):
    terms, rest = [], value
    for _ in range(3):
        terms.append(rest.astype(jnp.bfloat16))
        rest = rest - terms[-1].astype(jnp.float32)
    return terms


def pack_kernel(weight_ref, gain_ref, inputs_ref, sent_ref):
    count, rows, _ = sent_ref.shape
    units = weight_ref.shape[1] // count
    length = inputs_ref.shape[1]
    rest = units - length
    on_row = lax.broadcasted_iota(jnp.int32, (rows, rows), 0)
    on_col = lax.broadcasted_iota(jnp.int32, (rows, rows), 1)
    gain = jnp.sum(jnp.where(on_row == on_col, gain_ref[...], 0.0), axis=1, keepdims=True)
    lane = lax.broadcasted_iota(jnp.int32, (rows, length), 1)
    tail = jnp.zeros((rows, length), jnp.float32)
    for at, term in enumerate(three_terms(gain)):
        tail = jnp.where(lane == rest + at, term.astype(jnp.float32), tail)
    tail = tail[:, rest:].astype(jnp.bfloat16)
    for at in range(count):
        first = at * units
        sent_ref[at, :, 0:length] = weight_ref[:, first : first + length]
        sent_ref[at, :, length : 2 * length] = jnp.concatenate(
            [weight_ref[:, first + length : first + units], tail], axis=1
        )
        sent_ref[at, :, 2 * length : 3 * length] = inputs_ref[...]


def packed_blocks(weight, gain, inputs, count):
    rows, cols = weight.shape
    length = inputs.shape[1]
    group = 8
    return pl.pallas_call(
        pack_kernel,
        grid=(count // group,),
        in_specs=[
            pl.BlockSpec((rows, group * cols // count), lambda at: (0, at)),
            pl.BlockSpec((1, rows), lambda at: (0, 0)),
            pl.BlockSpec(inputs.shape, lambda at: (0, 0)),
        ],
        out_specs=pl.BlockSpec((group, rows, 3 * length), lambda at: (at, 0, 0)),
        out_shape=jax.ShapeDtypeStruct((count, rows, 3 * length), weight.dtype),
        cost_estimate=pl.CostEstimate(flops=0, bytes_accessed=5 * weight.size, transcendentals=0),
    )(weight, gain[None], inputs)


def column_kernel(weight_ref, blocks_ref):
    count, rows, padded = blocks_ref.shape
    units = weight_ref.shape[1] // count
    for at in range(count):
        blocks_ref[at] = jnp.concatenate(
            [
                weight_ref[:, at * units : (at + 1) * units],
                jnp.zeros((rows, padded - units), weight_ref.dtype),
            ],
            axis=1,
        )


def column_blocks(weight, count, lanes):
    rows, cols = weight.shape
    padded = -(-cols // count // lanes) * lanes
    group = 16
    return pl.pallas_call(
        column_kernel,
        grid=(count // group,),
        in_specs=[pl.BlockSpec((rows, group * cols // count), lambda at: (0, at))],
        out_specs=pl.BlockSpec((group, rows, padded), lambda at: (at, 0, 0)),
        out_shape=jax.ShapeDtypeStruct((count, rows, padded), weight.dtype),
        cost_estimate=pl.CostEstimate(flops=0, bytes_accessed=5 * weight.size, transcendentals=0),
    )(weight)


def dot_rows(left, right, **options):
    return lax.dot_general(left, right, contract_rows, preferred_element_type=jnp.float32, **options)


def dot_cols(left, right):
    return lax.dot_general(left, right, contract_cols, preferred_element_type=jnp.float32)


def dot_plain(left, right):
    return jnp.dot(left, right, preferred_element_type=jnp.float32)


def body(inputs, ln_gain, segment_ids, w_in, w_out, mom_in, mom_out, hess_in, hess_out, probe_seed):
    features, length = inputs.shape
    hidden_width = w_in.shape[1]
    planes = lax.axis_size(PLANE)
    deep = lax.axis_size(DEPTH)
    units = hidden_width // planes
    plane_rows = planes * features
    padded = -(-units // length) * length

    row_index = lax.axis_index(DP) * features + jnp.arange(features, dtype=jnp.int32)
    col_start = lax.axis_index(TENSOR) * hidden_width
    plane_index = (
        (jnp.arange(planes, dtype=jnp.int32)[:, None] * deep + lax.axis_index(DEPTH)) * features
        + jnp.arange(features, dtype=jnp.int32)[None, :]
    ).reshape(plane_rows)
    unit_start = col_start + lax.axis_index(PLANE) * units

    sent = packed_blocks(w_in, ln_gain, inputs, planes)
    sent, seeds, inputs, segment_ids, later_out = lax.optimization_barrier(
        (sent, probe_seed, inputs, segment_ids, w_out)
    )
    values = inputs.astype(jnp.float32)
    probes = (
        probe_signs(seeds[0], plane_index, unit_start, units),
        probe_signs(seeds[1], plane_index, unit_start, units),
        probe_signs(seeds[0], row_index, col_start, hidden_width),
        probe_signs(seeds[1], row_index, col_start, hidden_width),
    )
    target = jnp.concatenate([values[:, 1:], jnp.zeros((features, 1), jnp.float32)], axis=1)
    weights = token_weights(segment_ids)
    first_core = lax.axis_index(CORE) == 0
    got, out_blocks, probes, target, weights, first_core = lax.optimization_barrier(
        (swap(sent, PLANE), column_blocks(later_out, planes, length), probes, target, weights, first_core)
    )
    plane_probe_in, plane_probe_out, probe_in, probe_out = probes
    got = got.reshape(plane_rows, padded + length)
    plane_in = got[:, :units]
    gain_cols = got[:, units : units + 3]
    plane_gain = jnp.sum(gain_cols.astype(jnp.float32), axis=1, keepdims=True)
    plane_values = got[:, padded:].astype(jnp.float32)

    plane_mean = jnp.mean(plane_values, axis=0)
    plane_centered = plane_values - plane_mean
    plane_square = jnp.sum(plane_centered * plane_centered, axis=0)
    scaled = (plane_centered * plane_gain).astype(jnp.bfloat16)
    gain_sum = jnp.concatenate(
        [
            jnp.pad(jnp.sum(dot_rows(gain_cols, part), axis=0), (0, padded - units))
            for part in (plane_in, plane_probe_in)
        ]
    ).reshape(-1, length)
    extras = jnp.concatenate(
        [gain_sum.astype(jnp.bfloat16)]
        + [term[None] for term in three_terms(plane_mean) + three_terms(plane_square)],
        axis=0,
    )
    extra_rows = extras.shape[0]
    extras = jnp.pad(extras, ((0, -extra_rows % 16), (0, 0)))
    own = jnp.concatenate(
        [
            dot_rows(plane_in, scaled).astype(jnp.bfloat16),
            dot_rows(plane_probe_in, scaled).astype(jnp.bfloat16),
            extras,
        ],
        axis=0,
    )
    own, out_blocks = lax.optimization_barrier((own, out_blocks))
    every, plane_out = lax.optimization_barrier((turns(own), swap(out_blocks, PLANE)))
    plane_out = plane_out.reshape(plane_rows, padded)[:, :units]
    every = [part.astype(jnp.float32) for part in every]
    tails = jnp.stack([part[2 * units : 2 * units + extra_rows] for part in every])
    sums = tails[:, : 2 * padded // length].reshape(deep, 2, padded)[:, :, :units]
    stats = jnp.sum(tails[:, 2 * padded // length :].reshape(deep, 2, 3, length), axis=2)
    mean_val = jnp.mean(stats[:, 0], axis=0)
    apart = stats[:, 0] - mean_val
    variance = jnp.sum(stats[:, 1] + plane_rows * apart * apart, axis=0) / D
    scale = lax.rsqrt(variance + NORM_EPS)
    totals = sum(part[: 2 * units] for part in every)
    pre, pre_dot = (
        scale
        * (
            totals[at * units : (at + 1) * units]
            + dot_rows(sums[:, at], apart, precision=lax.Precision.HIGHEST)
        )
        for at in range(2)
    )

    act, slope, curve = gelu_parts(pre)
    both = spread(jnp.concatenate([act, slope * pre_dot], axis=0).astype(jnp.bfloat16), PLANE)
    hidden = both[:, :units].reshape(hidden_width, length)
    hidden_dot = both[:, units:].reshape(hidden_width, length)

    share = jnp.stack(
        [
            dot_plain(w_out, hidden),
            dot_plain(w_out, hidden_dot) + dot_plain(probe_out, hidden),
        ]
    ).astype(jnp.bfloat16)
    output, output_dot = jnp.sum(lax.all_gather(share, TENSOR).astype(jnp.float32), axis=0)
    cotangent = (weights * (output - target)).astype(jnp.bfloat16)
    cotangent_dot = (weights * output_dot).astype(jnp.bfloat16)

    held = spread(jnp.where(first_core, cotangent, cotangent_dot), PLANE).reshape(plane_rows, length)
    other = lax.ppermute(held, CORE, [(0, 1), (1, 0)])
    plane_cot = jnp.where(first_core, held, other)
    plane_cot_dot = jnp.where(first_core, other, held)
    own = jnp.concatenate(
        [
            dot_rows(plane_out, plane_cot),
            dot_rows(plane_out, plane_cot_dot) + dot_rows(plane_probe_out, plane_cot),
        ],
        axis=0,
    ).astype(jnp.bfloat16)
    own, cotangent, cotangent_dot = lax.optimization_barrier((own, cotangent, cotangent_dot))
    grad_out = dot_cols(cotangent, hidden)
    hvp_out = dot_cols(cotangent_dot, hidden) + dot_cols(cotangent, hidden_dot)
    outs = sophia_update(mom_out, hess_out, grad_out, hvp_out, probe_out)
    normed = ((values - mean_val) * scale * ln_gain[:, None]).astype(jnp.bfloat16)
    back_parts, outs, normed = lax.optimization_barrier((turns(own), outs, normed))
    back_total = sum(part.astype(jnp.float32) for part in back_parts)
    back, back_dot = back_total[:units], back_total[units:]
    grads = spread(
        jnp.concatenate(
            [slope * back, curve * pre_dot * back + slope * back_dot], axis=0
        ).astype(jnp.bfloat16),
        PLANE,
    )

    new_mom_in, new_hess_in, step_in = updated(normed, grads, probe_in, mom_in, hess_in)
    return (new_mom_in, new_hess_in, step_in) + tuple(outs)


def solution(mesh):
    torus = Mesh(mesh.devices.reshape(4, 4, 4, 2, 2), ("y", "x", "h", "l", "c"))
    matrix = P(DP, TENSOR)
    in_specs = (P(DP, None), P(DP), P()) + (matrix,) * 6 + (P(),)
    return jax.shard_map(
        body, mesh=torus, in_specs=in_specs, out_specs=(matrix,) * 6, check_vma=False
    )
```

```python
import jax
import jax.numpy as jnp
from jax import lax
from jax.experimental import pallas as pl
from jax.experimental.pallas import tpu as pltpu
from jax.sharding import Mesh, PartitionSpec as P

D = 7168
FF = 14336


BETA_ONE = 0.96
BETA_TWO = 0.99
SCALE_GAMMA = 0.05
FLOOR_EPS = 0.002
NORM_EPS = 1e-05
hash_factor = 73244475
contract_rows = (((0,), (0,)), ((), ()))
contract_cols = (((1,), (1,)), ((), ()))
PLANE = ("y", "x")
DEPTH = ("h",)
DP = PLANE + DEPTH
TENSOR = ("l", "c")
CORE = "c"


def mixing(words):
    words = (words ^ words >> 16 & 65535) * hash_factor
    words = (words ^ words >> 16 & 65535) * hash_factor
    return words ^ words >> 16 & 65535


def probe_signs(seed_word, rows_index, col_start, col_count):
    cols_index = col_start + jnp.arange(col_count, dtype=jnp.int32)[None, :]
    hashed = mixing(rows_index[:, None] * FF + cols_index ^ seed_word)
    return (1 - 2 * (hashed & 1)).astype(jnp.bfloat16)


def gelu_parts(preact):
    normal_cdf = 0.5 * (1.0 + lax.erf(preact * 0.7071067811865476))
    normal_pdf = jnp.exp(-0.5 * preact * preact) * 0.3989422804014327
    return (
        preact * normal_cdf,
        normal_cdf + preact * normal_pdf,
        normal_pdf * (2.0 - preact * preact),
    )


def token_weights(segment_ids):
    following = jnp.concatenate([segment_ids[1:], jnp.full((1,), -1, jnp.int32)])
    valid = (following == segment_ids).astype(jnp.float32)
    same_doc = (segment_ids[:, None] == segment_ids[None, :]).astype(jnp.float32)
    counts = jnp.dot(same_doc, valid, precision=lax.Precision.HIGHEST)
    return valid / jnp.maximum(counts, 1.0)


def sophia_update(moment_old, curve_old, gradient, product, probe):
    moment = BETA_ONE * moment_old.astype(jnp.float32) + (1.0 - BETA_ONE) * gradient
    curvature = (
        BETA_TWO * curve_old.astype(jnp.float32)
        + (1.0 - BETA_TWO) * probe.astype(jnp.float32) * product
    )
    stepped = jnp.clip(moment / jnp.maximum(SCALE_GAMMA * curvature, FLOOR_EPS), -1.0, 1.0)
    return (
        moment.astype(jnp.bfloat16),
        curvature.astype(jnp.bfloat16),
        stepped.astype(jnp.bfloat16),
    )


def update_kernel(normed_ref, grads_ref, probe_ref, mom_ref, hess_ref, new_mom, new_hess, step):
    count, both, _ = grads_ref.shape
    units = both // 2
    normed = normed_ref[...]
    pre_grad = jnp.concatenate([grads_ref[at, 0:units] for at in range(count)], axis=0)
    pre_grad_dot = jnp.concatenate([grads_ref[at, units:both] for at in range(count)], axis=0)
    new_mom[...], new_hess[...], step[...] = sophia_update(
        mom_ref[...],
        hess_ref[...],
        dot_cols(normed, pre_grad),
        dot_cols(normed, pre_grad_dot),
        probe_ref[...],
    )


def updated(normed, grads, probe, mom, hess):
    count, both, length = grads.shape
    rows, cols = mom.shape
    group = 8
    wide = pl.BlockSpec((rows, group * cols // count), lambda at: (0, at))
    return pl.pallas_call(
        update_kernel,
        grid=(count // group,),
        in_specs=[
            pl.BlockSpec(normed.shape, lambda at: (0, 0)),
            pl.BlockSpec((group, both, length), lambda at: (at, 0, 0)),
            wide,
            wide,
            wide,
        ],
        out_specs=[wide] * 3,
        out_shape=[jax.ShapeDtypeStruct(mom.shape, mom.dtype)] * 3,
        cost_estimate=pl.CostEstimate(
            flops=4 * rows * cols * length, bytes_accessed=16 * mom.size, transcendentals=0
        ),
        compiler_params=pltpu.CompilerParams(vmem_limit_bytes=32 * 1024 * 1024),
    )(normed, grads, probe, mom, hess)


def swap(blocks, axes):
    return lax.all_to_all(blocks, axes, 0, 0, tiled=True)


def spread(block, axes):
    count = lax.axis_size(axes)
    return swap(jnp.broadcast_to(block[None], (count,) + block.shape), axes)


def turns(block):
    count = lax.axis_size(DEPTH)
    return [block] + [
        lax.ppermute(block, DEPTH, [(at, (at + shift) % count) for at in range(count)])
        for shift in sorted(range(1, count), key=lambda turn: -min(turn, count - turn))
    ]


def three_terms(value):
    terms, rest = [], value
    for _ in range(3):
        terms.append(rest.astype(jnp.bfloat16))
        rest = rest - terms[-1].astype(jnp.float32)
    return terms


def pack_kernel(weight_ref, gain_ref, inputs_ref, sent_ref):
    count, rows, _ = sent_ref.shape
    units = weight_ref.shape[1] // count
    length = inputs_ref.shape[1]
    rest = units - length
    on_row = lax.broadcasted_iota(jnp.int32, (rows, rows), 0)
    on_col = lax.broadcasted_iota(jnp.int32, (rows, rows), 1)
    gain = jnp.sum(jnp.where(on_row == on_col, gain_ref[...], 0.0), axis=1, keepdims=True)
    lane = lax.broadcasted_iota(jnp.int32, (rows, length), 1)
    tail = jnp.zeros((rows, length), jnp.float32)
    for at, term in enumerate(three_terms(gain)):
        tail = jnp.where(lane == rest + at, term.astype(jnp.float32), tail)
    tail = tail[:, rest:].astype(jnp.bfloat16)
    for at in range(count):
        first = at * units
        sent_ref[at, :, 0:length] = weight_ref[:, first : first + length]
        sent_ref[at, :, length : 2 * length] = jnp.concatenate(
            [weight_ref[:, first + length : first + units], tail], axis=1
        )
        sent_ref[at, :, 2 * length : 3 * length] = inputs_ref[...]


def packed_blocks(weight, gain, inputs, count):
    rows, cols = weight.shape
    length = inputs.shape[1]
    group = 8
    return pl.pallas_call(
        pack_kernel,
        grid=(count // group,),
        in_specs=[
            pl.BlockSpec((rows, group * cols // count), lambda at: (0, at)),
            pl.BlockSpec((1, rows), lambda at: (0, 0)),
            pl.BlockSpec(inputs.shape, lambda at: (0, 0)),
        ],
        out_specs=pl.BlockSpec((group, rows, 3 * length), lambda at: (at, 0, 0)),
        out_shape=jax.ShapeDtypeStruct((count, rows, 3 * length), weight.dtype),
        cost_estimate=pl.CostEstimate(flops=0, bytes_accessed=5 * weight.size, transcendentals=0),
    )(weight, gain[None], inputs)


def column_kernel(weight_ref, blocks_ref):
    count, rows, padded = blocks_ref.shape
    units = weight_ref.shape[1] // count
    for at in range(count):
        blocks_ref[at] = jnp.concatenate(
            [
                weight_ref[:, at * units : (at + 1) * units],
                jnp.zeros((rows, padded - units), weight_ref.dtype),
            ],
            axis=1,
        )


def column_blocks(weight, count, lanes):
    rows, cols = weight.shape
    padded = -(-cols // count // lanes) * lanes
    group = 16
    return pl.pallas_call(
        column_kernel,
        grid=(count // group,),
        in_specs=[pl.BlockSpec((rows, group * cols // count), lambda at: (0, at))],
        out_specs=pl.BlockSpec((group, rows, padded), lambda at: (at, 0, 0)),
        out_shape=jax.ShapeDtypeStruct((count, rows, padded), weight.dtype),
        cost_estimate=pl.CostEstimate(flops=0, bytes_accessed=5 * weight.size, transcendentals=0),
    )(weight)


def dot_rows(left, right, **options):
    return lax.dot_general(left, right, contract_rows, preferred_element_type=jnp.float32, **options)


def dot_cols(left, right):
    return lax.dot_general(left, right, contract_cols, preferred_element_type=jnp.float32)


def dot_plain(left, right):
    return jnp.dot(left, right, preferred_element_type=jnp.float32)


def body(inputs, ln_gain, segment_ids, w_in, w_out, mom_in, mom_out, hess_in, hess_out, probe_seed):
    features, length = inputs.shape
    hidden_width = w_in.shape[1]
    planes = lax.axis_size(PLANE)
    deep = lax.axis_size(DEPTH)
    units = hidden_width // planes
    plane_rows = planes * features
    padded = -(-units // length) * length

    row_index = lax.axis_index(DP) * features + jnp.arange(features, dtype=jnp.int32)
    col_start = lax.axis_index(TENSOR) * hidden_width
    plane_index = (
        (jnp.arange(planes, dtype=jnp.int32)[:, None] * deep + lax.axis_index(DEPTH)) * features
        + jnp.arange(features, dtype=jnp.int32)[None, :]
    ).reshape(plane_rows)
    unit_start = col_start + lax.axis_index(PLANE) * units

    sent = packed_blocks(w_in, ln_gain, inputs, planes)
    sent, seeds, inputs, segment_ids, later_out = lax.optimization_barrier(
        (sent, probe_seed, inputs, segment_ids, w_out)
    )
    values = inputs.astype(jnp.float32)
    probes = (
        probe_signs(seeds[0], plane_index, unit_start, units),
        probe_signs(seeds[1], plane_index, unit_start, units),
        probe_signs(seeds[0], row_index, col_start, hidden_width),
        probe_signs(seeds[1], row_index, col_start, hidden_width),
    )
    target = jnp.concatenate([values[:, 1:], jnp.zeros((features, 1), jnp.float32)], axis=1)
    weights = token_weights(segment_ids)
    first_core = lax.axis_index(CORE) == 0
    got, out_blocks, probes, target, weights, first_core = lax.optimization_barrier(
        (swap(sent, PLANE), column_blocks(later_out, planes, length), probes, target, weights, first_core)
    )
    plane_probe_in, plane_probe_out, probe_in, probe_out = probes
    got = got.reshape(plane_rows, padded + length)
    plane_in = got[:, :units]
    gain_cols = got[:, units : units + 3]
    plane_gain = jnp.sum(gain_cols.astype(jnp.float32), axis=1, keepdims=True)
    plane_values = got[:, padded:].astype(jnp.float32)

    plane_mean = jnp.mean(plane_values, axis=0)
    plane_centered = plane_values - plane_mean
    plane_square = jnp.sum(plane_centered * plane_centered, axis=0)
    scaled = (plane_centered * plane_gain).astype(jnp.bfloat16)
    gain_sum = jnp.concatenate(
        [
            jnp.pad(jnp.sum(dot_rows(gain_cols, part), axis=0), (0, padded - units))
            for part in (plane_in, plane_probe_in)
        ]
    ).reshape(-1, length)
    extras = jnp.concatenate(
        [gain_sum.astype(jnp.bfloat16)]
        + [term[None] for term in three_terms(plane_mean) + three_terms(plane_square)],
        axis=0,
    )
    extra_rows = extras.shape[0]
    extras = jnp.pad(extras, ((0, -extra_rows % 16), (0, 0)))
    own = jnp.concatenate(
        [
            dot_rows(plane_in, scaled).astype(jnp.bfloat16),
            dot_rows(plane_probe_in, scaled).astype(jnp.bfloat16),
            extras,
        ],
        axis=0,
    )
    own, out_blocks = lax.optimization_barrier((own, out_blocks))
    every, plane_out = lax.optimization_barrier((turns(own), swap(out_blocks, PLANE)))
    plane_out = plane_out.reshape(plane_rows, padded)[:, :units]
    every = [part.astype(jnp.float32) for part in every]
    tails = jnp.stack([part[2 * units : 2 * units + extra_rows] for part in every])
    sums = tails[:, : 2 * padded // length].reshape(deep, 2, padded)[:, :, :units]
    stats = jnp.sum(tails[:, 2 * padded // length :].reshape(deep, 2, 3, length), axis=2)
    mean_val = jnp.mean(stats[:, 0], axis=0)
    apart = stats[:, 0] - mean_val
    variance = jnp.sum(stats[:, 1] + plane_rows * apart * apart, axis=0) / D
    scale = lax.rsqrt(variance + NORM_EPS)
    totals = sum(part[: 2 * units] for part in every)
    pre, pre_dot = (
        scale
        * (
            totals[at * units : (at + 1) * units]
            + dot_rows(sums[:, at], apart, precision=lax.Precision.HIGHEST)
        )
        for at in range(2)
    )

    act, slope, curve = gelu_parts(pre)
    both = spread(jnp.concatenate([act, slope * pre_dot], axis=0).astype(jnp.bfloat16), PLANE)
    hidden = both[:, :units].reshape(hidden_width, length)
    hidden_dot = both[:, units:].reshape(hidden_width, length)

    share = jnp.stack(
        [
            dot_plain(w_out, hidden),
            dot_plain(w_out, hidden_dot) + dot_plain(probe_out, hidden),
        ]
    ).astype(jnp.bfloat16)
    output, output_dot = jnp.sum(lax.all_gather(share, TENSOR).astype(jnp.float32), axis=0)
    cotangent = (weights * (output - target)).astype(jnp.bfloat16)
    cotangent_dot = (weights * output_dot).astype(jnp.bfloat16)

    held = spread(jnp.where(first_core, cotangent, cotangent_dot), PLANE).reshape(plane_rows, length)
    other = lax.ppermute(held, CORE, [(0, 1), (1, 0)])
    plane_cot = jnp.where(first_core, held, other)
    plane_cot_dot = jnp.where(first_core, other, held)
    own = jnp.concatenate(
        [
            dot_rows(plane_out, plane_cot),
            dot_rows(plane_out, plane_cot_dot) + dot_rows(plane_probe_out, plane_cot),
        ],
        axis=0,
    ).astype(jnp.bfloat16)
    own, cotangent, cotangent_dot = lax.optimization_barrier((own, cotangent, cotangent_dot))
    grad_out = dot_cols(cotangent, hidden)
    hvp_out = dot_cols(cotangent_dot, hidden) + dot_cols(cotangent, hidden_dot)
    outs = sophia_update(mom_out, hess_out, grad_out, hvp_out, probe_out)
    normed = ((values - mean_val) * scale * ln_gain[:, None]).astype(jnp.bfloat16)
    back_parts, outs, normed = lax.optimization_barrier((turns(own), outs, normed))
    back_total = sum(part.astype(jnp.float32) for part in back_parts)
    back, back_dot = back_total[:units], back_total[units:]
    grads = spread(
        jnp.concatenate(
            [slope * back, curve * pre_dot * back + slope * back_dot], axis=0
        ).astype(jnp.bfloat16),
        PLANE,
    )

    new_mom_in, new_hess_in, step_in = updated(normed, grads, probe_in, mom_in, hess_in)
    return (new_mom_in, new_hess_in, step_in) + tuple(outs)


def solution(mesh):
    torus = Mesh(mesh.devices.reshape(4, 4, 4, 2, 2), ("y", "x", "h", "l", "c"))
    matrix = P(DP, TENSOR)
    in_specs = (P(DP, None), P(DP), P()) + (matrix,) * 6 + (P(),)
    return jax.shard_map(
        body, mesh=torus, in_specs=in_specs, out_specs=(matrix,) * 6, check_vma=False
    )
```

```python
import jax
import jax.numpy as jnp
from jax import lax
from jax.experimental import pallas as pl
from jax.experimental.pallas import tpu as pltpu
from jax.sharding import Mesh, PartitionSpec as P

D = 7168
FF = 14336


BETA_ONE = 0.96
BETA_TWO = 0.99
SCALE_GAMMA = 0.05
FLOOR_EPS = 0.002
NORM_EPS = 1e-05
hash_factor = 73244475
contract_rows = (((0,), (0,)), ((), ()))
contract_cols = (((1,), (1,)), ((), ()))
PLANE = ("y", "x")
DEPTH = ("h",)
DP = PLANE + DEPTH
TENSOR = ("l", "c")
CORE = "c"


def mixing(words):
    words = (words ^ words >> 16 & 65535) * hash_factor
    words = (words ^ words >> 16 & 65535) * hash_factor
    return words ^ words >> 16 & 65535


def probe_signs(seed_word, rows_index, col_start, col_count):
    cols_index = col_start + jnp.arange(col_count, dtype=jnp.int32)[None, :]
    hashed = mixing(rows_index[:, None] * FF + cols_index ^ seed_word)
    return (1 - 2 * (hashed & 1)).astype(jnp.bfloat16)


def gelu_parts(preact):
    normal_cdf = 0.5 * (1.0 + lax.erf(preact * 0.7071067811865476))
    normal_pdf = jnp.exp(-0.5 * preact * preact) * 0.3989422804014327
    return (
        preact * normal_cdf,
        normal_cdf + preact * normal_pdf,
        normal_pdf * (2.0 - preact * preact),
    )


def token_weights(segment_ids):
    following = jnp.concatenate([segment_ids[1:], jnp.full((1,), -1, jnp.int32)])
    valid = (following == segment_ids).astype(jnp.float32)
    same_doc = (segment_ids[:, None] == segment_ids[None, :]).astype(jnp.float32)
    counts = jnp.dot(same_doc, valid, precision=lax.Precision.HIGHEST)
    return valid / jnp.maximum(counts, 1.0)


def sophia_update(moment_old, curve_old, gradient, product, probe):
    moment = BETA_ONE * moment_old.astype(jnp.float32) + (1.0 - BETA_ONE) * gradient
    curvature = (
        BETA_TWO * curve_old.astype(jnp.float32)
        + (1.0 - BETA_TWO) * probe.astype(jnp.float32) * product
    )
    stepped = jnp.clip(moment / jnp.maximum(SCALE_GAMMA * curvature, FLOOR_EPS), -1.0, 1.0)
    return (
        moment.astype(jnp.bfloat16),
        curvature.astype(jnp.bfloat16),
        stepped.astype(jnp.bfloat16),
    )


def update_kernel(normed_ref, grads_ref, probe_ref, mom_ref, hess_ref, new_mom, new_hess, step):
    count, both, _ = grads_ref.shape
    units = both // 2
    normed = normed_ref[...]
    pre_grad = jnp.concatenate([grads_ref[at, 0:units] for at in range(count)], axis=0)
    pre_grad_dot = jnp.concatenate([grads_ref[at, units:both] for at in range(count)], axis=0)
    new_mom[...], new_hess[...], step[...] = sophia_update(
        mom_ref[...],
        hess_ref[...],
        dot_cols(normed, pre_grad),
        dot_cols(normed, pre_grad_dot),
        probe_ref[...],
    )


def updated(normed, grads, probe, mom, hess):
    count, both, length = grads.shape
    rows, cols = mom.shape
    group = 8
    wide = pl.BlockSpec((rows, group * cols // count), lambda at: (0, at))
    return pl.pallas_call(
        update_kernel,
        grid=(count // group,),
        in_specs=[
            pl.BlockSpec(normed.shape, lambda at: (0, 0)),
            pl.BlockSpec((group, both, length), lambda at: (at, 0, 0)),
            wide,
            wide,
            wide,
        ],
        out_specs=[wide] * 3,
        out_shape=[jax.ShapeDtypeStruct(mom.shape, mom.dtype)] * 3,
        cost_estimate=pl.CostEstimate(
            flops=4 * rows * cols * length, bytes_accessed=16 * mom.size, transcendentals=0
        ),
        compiler_params=pltpu.CompilerParams(vmem_limit_bytes=32 * 1024 * 1024),
    )(normed, grads, probe, mom, hess)


def swap(blocks, axes):
    return lax.all_to_all(blocks, axes, 0, 0, tiled=True)


def spread(block, axes):
    count = lax.axis_size(axes)
    return swap(jnp.broadcast_to(block[None], (count,) + block.shape), axes)


def turns(block):
    count = lax.axis_size(DEPTH)
    return [block] + [
        lax.ppermute(block, DEPTH, [(at, (at + shift) % count) for at in range(count)])
        for shift in sorted(range(1, count), key=lambda turn: -min(turn, count - turn))
    ]


def three_terms(value):
    terms, rest = [], value
    for _ in range(3):
        terms.append(rest.astype(jnp.bfloat16))
        rest = rest - terms[-1].astype(jnp.float32)
    return terms


def pack_kernel(weight_ref, gain_ref, inputs_ref, sent_ref):
    count, rows, _ = sent_ref.shape
    units = weight_ref.shape[1] // count
    length = inputs_ref.shape[1]
    rest = units - length
    on_row = lax.broadcasted_iota(jnp.int32, (rows, rows), 0)
    on_col = lax.broadcasted_iota(jnp.int32, (rows, rows), 1)
    gain = jnp.sum(jnp.where(on_row == on_col, gain_ref[...], 0.0), axis=1, keepdims=True)
    lane = lax.broadcasted_iota(jnp.int32, (rows, length), 1)
    tail = jnp.zeros((rows, length), jnp.float32)
    for at, term in enumerate(three_terms(gain)):
        tail = jnp.where(lane == rest + at, term.astype(jnp.float32), tail)
    tail = tail[:, rest:].astype(jnp.bfloat16)
    for at in range(count):
        first = at * units
        sent_ref[at, :, 0:length] = weight_ref[:, first : first + length]
        sent_ref[at, :, length : 2 * length] = jnp.concatenate(
            [weight_ref[:, first + length : first + units], tail], axis=1
        )
        sent_ref[at, :, 2 * length : 3 * length] = inputs_ref[...]


def packed_blocks(weight, gain, inputs, count):
    rows, cols = weight.shape
    length = inputs.shape[1]
    group = 8
    return pl.pallas_call(
        pack_kernel,
        grid=(count // group,),
        in_specs=[
            pl.BlockSpec((rows, group * cols // count), lambda at: (0, at)),
            pl.BlockSpec((1, rows), lambda at: (0, 0)),
            pl.BlockSpec(inputs.shape, lambda at: (0, 0)),
        ],
        out_specs=pl.BlockSpec((group, rows, 3 * length), lambda at: (at, 0, 0)),
        out_shape=jax.ShapeDtypeStruct((count, rows, 3 * length), weight.dtype),
        cost_estimate=pl.CostEstimate(flops=0, bytes_accessed=5 * weight.size, transcendentals=0),
    )(weight, gain[None], inputs)


def column_kernel(weight_ref, blocks_ref):
    count, rows, padded = blocks_ref.shape
    units = weight_ref.shape[1] // count
    for at in range(count):
        blocks_ref[at] = jnp.concatenate(
            [
                weight_ref[:, at * units : (at + 1) * units],
                jnp.zeros((rows, padded - units), weight_ref.dtype),
            ],
            axis=1,
        )


def column_blocks(weight, count, lanes):
    rows, cols = weight.shape
    padded = -(-cols // count // lanes) * lanes
    group = 16
    return pl.pallas_call(
        column_kernel,
        grid=(count // group,),
        in_specs=[pl.BlockSpec((rows, group * cols // count), lambda at: (0, at))],
        out_specs=pl.BlockSpec((group, rows, padded), lambda at: (at, 0, 0)),
        out_shape=jax.ShapeDtypeStruct((count, rows, padded), weight.dtype),
        cost_estimate=pl.CostEstimate(flops=0, bytes_accessed=5 * weight.size, transcendentals=0),
    )(weight)


def dot_rows(left, right, **options):
    return lax.dot_general(left, right, contract_rows, preferred_element_type=jnp.float32, **options)


def dot_cols(left, right):
    return lax.dot_general(left, right, contract_cols, preferred_element_type=jnp.float32)


def dot_plain(left, right):
    return jnp.dot(left, right, preferred_element_type=jnp.float32)


def body(inputs, ln_gain, segment_ids, w_in, w_out, mom_in, mom_out, hess_in, hess_out, probe_seed):
    features, length = inputs.shape
    hidden_width = w_in.shape[1]
    planes = lax.axis_size(PLANE)
    deep = lax.axis_size(DEPTH)
    units = hidden_width // planes
    plane_rows = planes * features
    padded = -(-units // length) * length

    row_index = lax.axis_index(DP) * features + jnp.arange(features, dtype=jnp.int32)
    col_start = lax.axis_index(TENSOR) * hidden_width
    plane_index = (
        (jnp.arange(planes, dtype=jnp.int32)[:, None] * deep + lax.axis_index(DEPTH)) * features
        + jnp.arange(features, dtype=jnp.int32)[None, :]
    ).reshape(plane_rows)
    unit_start = col_start + lax.axis_index(PLANE) * units

    sent = packed_blocks(w_in, ln_gain, inputs, planes)
    sent, seeds, inputs, segment_ids, later_out = lax.optimization_barrier(
        (sent, probe_seed, inputs, segment_ids, w_out)
    )
    values = inputs.astype(jnp.float32)
    probes = (
        probe_signs(seeds[0], plane_index, unit_start, units),
        probe_signs(seeds[1], plane_index, unit_start, units),
        probe_signs(seeds[0], row_index, col_start, hidden_width),
        probe_signs(seeds[1], row_index, col_start, hidden_width),
    )
    target = jnp.concatenate([values[:, 1:], jnp.zeros((features, 1), jnp.float32)], axis=1)
    weights = token_weights(segment_ids)
    first_core = lax.axis_index(CORE) == 0
    got, out_blocks, probes, target, weights, first_core = lax.optimization_barrier(
        (swap(sent, PLANE), column_blocks(later_out, planes, length), probes, target, weights, first_core)
    )
    plane_probe_in, plane_probe_out, probe_in, probe_out = probes
    got = got.reshape(plane_rows, padded + length)
    plane_in = got[:, :units]
    gain_cols = got[:, units : units + 3]
    plane_gain = jnp.sum(gain_cols.astype(jnp.float32), axis=1, keepdims=True)
    plane_values = got[:, padded:].astype(jnp.float32)

    plane_mean = jnp.mean(plane_values, axis=0)
    plane_centered = plane_values - plane_mean
    plane_square = jnp.sum(plane_centered * plane_centered, axis=0)
    scaled = (plane_centered * plane_gain).astype(jnp.bfloat16)
    gain_sum = jnp.concatenate(
        [
            jnp.pad(jnp.sum(dot_rows(gain_cols, part), axis=0), (0, padded - units))
            for part in (plane_in, plane_probe_in)
        ]
    ).reshape(-1, length)
    extras = jnp.concatenate(
        [gain_sum.astype(jnp.bfloat16)]
        + [term[None] for term in three_terms(plane_mean) + three_terms(plane_square)],
        axis=0,
    )
    extra_rows = extras.shape[0]
    extras = jnp.pad(extras, ((0, -extra_rows % 16), (0, 0)))
    own = jnp.concatenate(
        [
            dot_rows(plane_in, scaled).astype(jnp.bfloat16),
            dot_rows(plane_probe_in, scaled).astype(jnp.bfloat16),
            extras,
        ],
        axis=0,
    )
    own, out_blocks = lax.optimization_barrier((own, out_blocks))
    every, plane_out = lax.optimization_barrier((turns(own), swap(out_blocks, PLANE)))
    plane_out = plane_out.reshape(plane_rows, padded)[:, :units]
    every = [part.astype(jnp.float32) for part in every]
    tails = jnp.stack([part[2 * units : 2 * units + extra_rows] for part in every])
    sums = tails[:, : 2 * padded // length].reshape(deep, 2, padded)[:, :, :units]
    stats = jnp.sum(tails[:, 2 * padded // length :].reshape(deep, 2, 3, length), axis=2)
    mean_val = jnp.mean(stats[:, 0], axis=0)
    apart = stats[:, 0] - mean_val
    variance = jnp.sum(stats[:, 1] + plane_rows * apart * apart, axis=0) / D
    scale = lax.rsqrt(variance + NORM_EPS)
    totals = sum(part[: 2 * units] for part in every)
    pre, pre_dot = (
        scale
        * (
            totals[at * units : (at + 1) * units]
            + dot_rows(sums[:, at], apart, precision=lax.Precision.HIGHEST)
        )
        for at in range(2)
    )

    act, slope, curve = gelu_parts(pre)
    both = spread(jnp.concatenate([act, slope * pre_dot], axis=0).astype(jnp.bfloat16), PLANE)
    hidden = both[:, :units].reshape(hidden_width, length)
    hidden_dot = both[:, units:].reshape(hidden_width, length)

    share = jnp.stack(
        [
            dot_plain(w_out, hidden),
            dot_plain(w_out, hidden_dot) + dot_plain(probe_out, hidden),
        ]
    ).astype(jnp.bfloat16)
    output, output_dot = jnp.sum(lax.all_gather(share, TENSOR).astype(jnp.float32), axis=0)
    cotangent = (weights * (output - target)).astype(jnp.bfloat16)
    cotangent_dot = (weights * output_dot).astype(jnp.bfloat16)

    held = spread(jnp.where(first_core, cotangent, cotangent_dot), PLANE).reshape(plane_rows, length)
    other = lax.ppermute(held, CORE, [(0, 1), (1, 0)])
    plane_cot = jnp.where(first_core, held, other)
    from_held, from_other = dot_rows(plane_out, held), dot_rows(plane_out, other)
    own = jnp.concatenate(
        [
            jnp.where(first_core, from_held, from_other),
            jnp.where(first_core, from_other, from_held) + dot_rows(plane_probe_out, plane_cot),
        ],
        axis=0,
    ).astype(jnp.bfloat16)
    own, cotangent, cotangent_dot = lax.optimization_barrier((own, cotangent, cotangent_dot))
    grad_out = dot_cols(cotangent, hidden)
    hvp_out = dot_cols(cotangent_dot, hidden) + dot_cols(cotangent, hidden_dot)
    outs = sophia_update(mom_out, hess_out, grad_out, hvp_out, probe_out)
    normed = ((values - mean_val) * scale * ln_gain[:, None]).astype(jnp.bfloat16)
    back_parts, outs, normed = lax.optimization_barrier((turns(own), outs, normed))
    back_total = sum(part.astype(jnp.float32) for part in back_parts)
    back, back_dot = back_total[:units], back_total[units:]
    grads = spread(
        jnp.concatenate(
            [slope * back, curve * pre_dot * back + slope * back_dot], axis=0
        ).astype(jnp.bfloat16),
        PLANE,
    )

    new_mom_in, new_hess_in, step_in = updated(normed, grads, probe_in, mom_in, hess_in)
    return (new_mom_in, new_hess_in, step_in) + tuple(outs)


def solution(mesh):
    torus = Mesh(mesh.devices.reshape(4, 4, 4, 2, 2), ("y", "x", "h", "l", "c"))
    matrix = P(DP, TENSOR)
    in_specs = (P(DP, None), P(DP), P()) + (matrix,) * 6 + (P(),)
    return jax.shard_map(
        body, mesh=torus, in_specs=in_specs, out_specs=(matrix,) * 6, check_vma=False
    )
```
